32 devices in a mesh: space: 16 (over z, y, core), chan: 2 (over x).
Axes of the slice: x: 2, y: 2, z: 4, core: 2. Of those that a mesh axis runs over, the one named last changes fastest.
Arguments:
- features: bfloat16 [1, 128, 32, 2048], P(None, 'chan', 'space'), may hold values from -6 to 6
- top_map: int32 [16, 2048], P('space'), may hold values from 0 to 2048, as said below
- bottom_map: int32 [16, 2048], P('space'), may hold values from 0 to 2048, as said below
- first_weight: bfloat16 [128, 3, 3, 128], P('chan'), may hold values from -0.1875 to 0.1875
- first_bias: float32 [128], P('chan'), may hold values from -3 to 3
- second_weight: bfloat16 [256, 3, 3, 128], P('chan'), may hold values from -0.1875 to 0.1875
- second_bias: float32 [256], P('chan'), may hold values from -3 to 3
Outputs:
- hidden: bfloat16 [1, 128, 32, 2048], P(None, 'chan', 'space')
- coarse: bfloat16 [1, 256, 16, 1024], P(None, 'chan', 'space')
The draws below stay inside these ranges and needn't reach their ends.
Inputs may be any that keep to these rules, and one draw needn't show every extreme that they name: `top_map`: each entry of row s, column k is k - 1, k or k + 1 taken modulo 2048, or 2048 for a missing neighbour at a face corner; exactly 4 entries of each row equal 2048. `bottom_map`: each entry of row s, column k is k - 1, k or k + 1 taken modulo 2048, or 2048 for a missing neighbour at a face corner; exactly 4 entries of each row equal 2048.
All inputs are finite; a program needn't handle non-finite values.
Results may differ from the reference program's by a relative error of at most 0.012.
Values may be sent and summed in bfloat16 or wider, within the bound.
A program may use at most 64 MiB of HBM per device.

```python
from functools import partial
import jax
import jax.numpy as jnp
from jax import lax

C = 128
C2 = 256
CYCLE = 2048
MEMBERS = 1
TILES = 16
CYCLES = 32


def corner_columns(corner_key):
    return jax.random.permutation(corner_key, CYCLE)[:4]


def rim_table(key):
    shift_key, corner_key = jax.random.split(key)
    shifts = jax.random.randint(shift_key, (TILES, CYCLE), -1, 2)
    columns = (jnp.arange(CYCLE)[None, :] + shifts) % CYCLE
    corner_keys = jax.random.split(corner_key, TILES)
    corners = jax.vmap(corner_columns)(corner_keys)
    marked = jnp.any(jnp.arange(CYCLE)[None, None, :] == corners[:, :, None], axis=1)
    return jnp.where(marked, CYCLE, columns).astype(jnp.int32)


def draw_top_map(key, part):
    return rim_table(jax.random.fold_in(key, 11))


def draw_bottom_map(key, part):
    return rim_table(jax.random.fold_in(key, 23))


def shard_levels(own_key, dims, pieces, least, top_value):
    gain = 1.0
    for dim, shards_of in pieces:
        steps = jax.random.uniform(jax.random.fold_in(jax.random.fold_in(own_key, 6), dim), (shards_of,), jnp.float32, least / len(pieces), top_value / len(pieces))
        gain = gain * jnp.repeat(jnp.exp(steps), dims[dim] // shards_of).reshape((-1,) + (1,) * (len(dims) - 1 - dim))
    return gain


def centred(stream_key, shape, spread, reach, pieces=(), held_as=jnp.bfloat16):
    drawn = spread * jax.random.normal(stream_key, shape, jnp.float32)
    if pieces:
        drawn = drawn * shard_levels(stream_key, shape, pieces, -0.22, 0.18)
    return jnp.clip(drawn, -reach, reach).astype(held_as)


def setup_inputs(seed: int = 0) -> dict:
    key_of = jax.random.split(jax.random.key(seed), 8)
    features = centred(key_of[0], (MEMBERS, C, CYCLES, CYCLE), 1.0, 6.0, ((1, 2), (2, 16)))
    top_map = draw_top_map(jax.random.fold_in(key_of[7], 71), 0)
    bottom_map = draw_bottom_map(jax.random.fold_in(key_of[7], 71), 0)
    first_weight = centred(key_of[3], (C, 3, 3, C), (9 * C) ** -0.5, 0.1875, ((0, 2),))
    first_bias = centred(key_of[4], (C,), 0.5, 3.0, ((0, 2),), jnp.float32)
    second_weight = centred(key_of[5], (C2, 3, 3, C), (9 * C) ** -0.5, 0.1875, ((0, 2),))
    second_bias = centred(key_of[6], (C2,), 0.5, 3.0, ((0, 2),), jnp.float32)
    return {"features": features, "top_map": top_map, "bottom_map": bottom_map, "first_weight": first_weight, "first_bias": first_bias, "second_weight": second_weight, "second_bias": second_bias}


def remap_rows(source_rows, table):
    zero_col = jnp.zeros(source_rows.shape[:-1] + (1,), source_rows.dtype)
    extended = jnp.concatenate([source_rows, zero_col], axis=-1)
    index = jnp.broadcast_to(table, source_rows.shape).astype(jnp.int32)
    return jnp.take_along_axis(extended, index, axis=-1)


def first_layer(sample, top_map, bottom_map, first_weight, first_bias):
    channels, cycle_count, cycle_width = sample.shape
    tile_count = top_map.shape[0]
    per_tile = cycle_count // tile_count
    band_rows = sample.reshape(channels, tile_count, per_tile, cycle_width)
    zero_row = jnp.zeros((channels, 1, cycle_width), sample.dtype)
    above_row = remap_rows(jnp.concatenate([zero_row, band_rows[:, :-1, -1, :]], 1), top_map)
    below_row = remap_rows(jnp.concatenate([band_rows[:, 1:, 0, :], zero_row], 1), bottom_map)
    padded = jnp.concatenate([above_row[:, :, None], band_rows, below_row[:, :, None]], 2).astype(jnp.float32)
    weight = first_weight.astype(jnp.float32)
    totals = jnp.zeros((weight.shape[0], tile_count, per_tile, cycle_width), jnp.float32)
    for row_step in range(3):
        for col_step in range(3):
            shifted = jnp.roll(padded[:, :, row_step:row_step + per_tile, :], 1 - col_step, axis=3)
            totals = totals + jnp.einsum("oc,csrw->osrw", weight[:, row_step, col_step, :], shifted)
    result = jax.nn.gelu(totals + first_bias.astype(jnp.float32)[:, None, None, None]).astype(jnp.bfloat16)
    return result.reshape(-1, cycle_count, cycle_width)


def second_layer(sample, top_map, second_weight, second_bias):
    channels, cycle_count, cycle_width = sample.shape
    tile_count = top_map.shape[0]
    per_tile = cycle_count // tile_count
    band_rows = sample.reshape(channels, tile_count, per_tile, cycle_width)
    zero_row = jnp.zeros((channels, 1, cycle_width), sample.dtype)
    above_row = remap_rows(jnp.concatenate([zero_row, band_rows[:, :-1, -1, :]], 1), top_map)
    stacked = jnp.concatenate([above_row[:, :, None], band_rows], 2).astype(jnp.float32)
    weight = second_weight.astype(jnp.float32)
    totals = jnp.zeros((weight.shape[0], tile_count, per_tile // 2, cycle_width // 2), jnp.float32)
    for row_step in range(3):
        for col_step in range(3):
            picked = jnp.roll(stacked[:, :, row_step:row_step + per_tile:2, :], 1 - col_step, axis=3)[..., ::2]
            totals = totals + jnp.einsum("oc,csrw->osrw", weight[:, row_step, col_step, :], picked)
    result = jax.nn.gelu(totals + second_bias.astype(jnp.float32)[:, None, None, None]).astype(jnp.bfloat16)
    return result.reshape(-1, cycle_count // 2, cycle_width // 2)


def reference(features, top_map, bottom_map, first_weight, first_bias, second_weight, second_bias):
    hidden = lax.map(partial(first_layer, top_map=top_map, bottom_map=bottom_map, first_weight=first_weight, first_bias=first_bias), features)
    coarse = lax.map(partial(second_layer, top_map=top_map, second_weight=second_weight, second_bias=second_bias), hidden)
    return (hidden, coarse)
```

```python
import functools

import jax
import jax.numpy as jnp
from jax import lax
from jax.experimental import pallas as pl
from jax.experimental.pallas import tpu as pltpu
from jax.sharding import PartitionSpec as P

MESH = pl.DeviceIdType.MESH
BF16 = jnp.bfloat16
F32 = jnp.float32
CHUNKS = 4


def gelu(v):
    return 0.5 * v * (1.0 + jnp.tanh(0.7978845608028654 * (v + 0.044715 * (v * v * v))))


def remap(raw, table):
    width = raw.shape[1]
    column = lax.broadcasted_iota(jnp.int32, (1, width), 1)
    before = jnp.where(column == 0, width - 1, column - 1)
    after = jnp.where(column == width - 1, 0, column + 1)
    pick = jnp.where(table == column, 1, jnp.where(table == before, 2, jnp.where(table == after, 3, 0)))
    pick = jnp.broadcast_to(pick, raw.shape)
    value = raw.astype(F32)
    found = jnp.where(pick == 1, value, 0.0)
    found = jnp.where(pick == 2, pltpu.roll(value, 1, 1), found)
    found = jnp.where(pick == 3, pltpu.roll(value, width - 1, 1), found)
    return found.astype(BF16)


def kernel(
    space, chan, x_ref, top_ref, bottom_ref, w1_ref, b1_ref, w2_ref, b2_ref, hidden_ref, coarse_ref,
    padded, upper, lower, wide, totals, rim, halves, w2_all, part_out, part_in,
    x_send, x_recv, up_send, up_recv, low_send, low_recv, rim_send, rim_recv, w_send, w_recv, p_send, p_recv,
):
    s = lax.axis_index("space")
    j = lax.axis_index("chan")
    _, c, width = x_ref.shape
    o = w1_ref.shape[1]
    channels = w1_ref.shape[2]
    o2 = w2_ref.shape[4]
    half = width // 2
    step = width // CHUNKS
    has_above = s > 0
    has_below = s < space - 1

    def peer(k):
        return lax.rem(j + k, chan)

    def source(k):
        return lax.rem(j + chan - k, chan)

    def remote(src, dst, send, recv, where):
        return pltpu.make_async_remote_copy(
            src_ref=src, dst_ref=dst, send_sem=send, recv_sem=recv, device_id=where, device_id_type=MESH
        )

    barrier = pltpu.get_barrier_semaphore()
    for k in range(1, chan):
        pl.semaphore_signal(barrier, inc=1, device_id=(s, peer(k)), device_id_type=MESH)

    @pl.when(has_above)
    def _():
        pl.semaphore_signal(barrier, inc=1, device_id=(s - 1, j), device_id_type=MESH)

    @pl.when(has_below)
    def _():
        pl.semaphore_signal(barrier, inc=1, device_id=(s + 1, j), device_id_type=MESH)

    pl.semaphore_wait(barrier, chan - 1 + jnp.where(has_above, 1, 0) + jnp.where(has_below, 1, 0))

    def columns(q):
        return pl.ds(q * step, step)

    def x_copy(k, q):
        return remote(
            x_ref.at[:, :, columns(q)], padded.at[1:3, j, :, columns(q)],
            x_send.at[k, q], x_recv.at[k, q], (s, peer(k)),
        )

    def w_copy(k):
        return remote(w2_ref.at[peer(k)], w2_all.at[j], w_send.at[k], w_recv.at[k], (s, peer(k)))

    def up_copy(src, block, k, q):
        return remote(src, upper.at[block, :, columns(q)], up_send.at[k, q], up_recv.at[k, q], (s + 1, j))

    def low_copy(src, block, k, q):
        return remote(src, lower.at[block, :, columns(q)], low_send.at[k, q], low_recv.at[k, q], (s - 1, j))

    def up_of(k, q):
        if k == 0:
            return up_copy(x_ref.at[1, :, columns(q)], j, 0, q)
        return up_copy(padded.at[2, source(k), :, columns(q)], source(k), k, q)

    def low_of(k, q):
        if k == 0:
            return low_copy(x_ref.at[0, :, columns(q)], j, 0, q)
        return low_copy(padded.at[1, source(k), :, columns(q)], source(k), k, q)

    def pass_on(k, q):
        @pl.when(has_below)
        def _():
            up_of(k, q).start()

        @pl.when(has_above)
        def _():
            low_of(k, q).start()

    for q in range(CHUNKS):
        for k in range(1, chan):
            x_copy(k, q).start()
    for q in range(CHUNKS):
        pass_on(0, q)
    for k in range(1, chan):
        w_copy(k).start()

    padded[1, j] = x_ref[0]
    padded[2, j] = x_ref[1]
    w2_all[j] = w2_ref[j]
    wide[...] = jnp.zeros_like(wide)
    for r in range(2):
        for a in range(3):
            for b in range(3):
                wide[(r * 3 + b) * o : (r * 3 + b + 1) * o, (r + a) * channels : (r + a + 1) * channels] = w1_ref[a * 3 + b]

    @pl.when(s == 0)
    def _():
        upper[...] = jnp.zeros_like(upper)
        rim[...] = jnp.zeros_like(rim)

    @pl.when(s == space - 1)
    def _():
        lower[...] = jnp.zeros_like(lower)

    for q in range(CHUNKS):
        for k in range(1, chan):
            x_copy(k, q).wait_recv()
            pass_on(k, q)

    for k in range(chan):
        @pl.when(has_above)
        def _():
            for q in range(CHUNKS):
                up_of(k, q).wait_recv()

        @pl.when(has_below)
        def _():
            for q in range(CHUNKS):
                low_of(k, q).wait_recv()

        padded[0, source(k)] = remap(upper[source(k)], top_ref[...])
        padded[3, source(k)] = remap(lower[source(k)], bottom_ref[...])

    def rim_copy():
        return remote(hidden_ref.at[1], rim, rim_send, rim_recv, (s + 1, j))

    spread = 256
    place = lax.broadcasted_iota(jnp.int32, (spread, spread), 0)
    wanted = lax.broadcasted_iota(jnp.int32, (spread, spread), 1)
    wanted = jnp.where(wanted < spread // 2, 2 * wanted, 2 * wanted - spread + 1)
    picker = jnp.where(place == wanted, 1.0, 0.0).astype(BF16)

    def split_columns(row, at):
        for block in range(width // spread):
            both = jnp.dot(row[:, block * spread : (block + 1) * spread], picker, preferred_element_type=F32).astype(BF16)
            here = slice(block * (spread // 2), (block + 1) * (spread // 2))
            halves[0, at, :, here] = both[:, : spread // 2]
            halves[1, at, :, here] = both[:, spread // 2 :]

    for r in (1, 0):
        first = r * channels
        taps = wide[r * 3 * o : (r + 1) * 3 * o, first : first + 3 * channels]
        for q in range(CHUNKS):
            stack = padded[r : r + 3, :, :, q * step : (q + 1) * step].reshape(3 * channels, step)
            totals[:, q * step : (q + 1) * step] = jnp.dot(taps, stack, preferred_element_type=F32)
        pre = (
            pltpu.roll(totals[:o], 1, 1) + totals[o : 2 * o] + pltpu.roll(totals[2 * o :], width - 1, 1) + b1_ref[...]
        )
        hidden_ref[r] = gelu(pre).astype(BF16)
        if r == 1:
            @pl.when(has_below)
            def _():
                rim_copy().start()

    split_columns(hidden_ref[0], 1)
    split_columns(hidden_ref[1], 2)
    for k in range(1, chan):
        w_copy(k).wait_recv()

    @pl.when(has_above)
    def _():
        rim_copy().wait_recv()

    split_columns(remap(rim[...], top_ref[...]), 0)

    even = halves[0].reshape(3 * c, half)
    odd = halves[1].reshape(3 * c, half)

    def product(owner, tap, data):
        weight = w2_all[owner, tap].reshape(3 * c, o2)
        return lax.dot_general(weight, data, (((0,), (0,)), ((), ())), preferred_element_type=F32)

    def partial(owner):
        return product(owner, 1, even) + product(owner, 2, odd) + pltpu.roll(product(owner, 0, odd), 1, 1)

    def p_copy(k):
        return remote(part_out.at[k], part_in.at[k], p_send.at[k], p_recv.at[k], (s, peer(k)))

    for k in range(1, chan):
        part_out[k] = partial(peer(k)).astype(BF16)
        p_copy(k).start()
    total = partial(j) + b2_ref[...]
    for k in range(1, chan):
        p_copy(k).wait_recv()
        total = total + part_in[k].astype(F32)
    coarse_ref[...] = gelu(total).astype(BF16)

    for k in range(1, chan):
        for q in range(CHUNKS):
            x_copy(k, q).wait_send()
        w_copy(k).wait_send()
        p_copy(k).wait_send()

    @pl.when(has_below)
    def _():
        for k in range(chan):
            for q in range(CHUNKS):
                up_of(k, q).wait_send()
        rim_copy().wait_send()

    @pl.when(has_above)
    def _():
        for k in range(chan):
            for q in range(CHUNKS):
                low_of(k, q).wait_send()


def per_device(space, chan, features, top_map, bottom_map, first_weight, first_bias, second_weight, second_bias):
    _, c, rows, width = features.shape
    o, _, _, channels = first_weight.shape
    o2 = second_weight.shape[0]
    half = width // 2
    x = jnp.transpose(features[0], (1, 0, 2))
    w1 = jnp.transpose(first_weight.reshape(o, 9, channels), (1, 0, 2))
    w2 = jnp.transpose(second_weight.reshape(o2, 3, 3, chan, c), (3, 2, 1, 4, 0))
    dma = pltpu.SemaphoreType.DMA
    hidden, coarse = pl.pallas_call(
        functools.partial(kernel, space, chan),
        out_shape=(
            jax.ShapeDtypeStruct((rows, o, width), BF16),
            jax.ShapeDtypeStruct((o2, half), BF16),
        ),
        in_specs=[pl.BlockSpec(memory_space=pltpu.VMEM)] * 7,
        out_specs=(pl.BlockSpec(memory_space=pltpu.VMEM),) * 2,
        scratch_shapes=[
            pltpu.VMEM((4, chan, c, width), BF16),
            pltpu.VMEM((chan, c, width), BF16),
            pltpu.VMEM((chan, c, width), BF16),
            pltpu.VMEM((6 * o, 4 * channels), BF16),
            pltpu.VMEM((3 * o, width), F32),
            pltpu.VMEM((o, width), BF16),
            pltpu.VMEM((2, 3, o, half), BF16),
            pltpu.VMEM((chan, 3, 3, c, o2), BF16),
            pltpu.VMEM((chan, o2, half), BF16),
            pltpu.VMEM((chan, o2, half), BF16),
            dma((chan, CHUNKS)),
            dma((chan, CHUNKS)),
            dma((chan, CHUNKS)),
            dma((chan, CHUNKS)),
            dma((chan, CHUNKS)),
            dma((chan, CHUNKS)),
            dma,
            dma,
            dma((chan,)),
            dma((chan,)),
            dma((chan,)),
            dma((chan,)),
        ],
        compiler_params=pltpu.CompilerParams(
            collective_id=0, has_side_effects=True, vmem_limit_bytes=40 * 1024 * 1024
        ),
    )(x, top_map, bottom_map, w1, first_bias[:, None], w2, second_bias[:, None])
    return jnp.transpose(hidden, (1, 0, 2))[None], coarse[None, :, None, :]


def solution(mesh):
    placed = (
        P(None, "chan", "space", None),
        P("space", None),
        P("space", None),
        P("chan", None, None, None),
        P("chan"),
        P("chan", None, None, None),
        P("chan"),
    )
    return jax.shard_map(
        functools.partial(per_device, mesh.shape["space"], mesh.shape["chan"]),
        mesh=mesh,
        in_specs=placed,
        out_specs=(P(None, "chan", "space", None), P(None, "chan", "space", None)),
        check_vma=False,
    )
```

```python
import functools

import jax
import jax.numpy as jnp
from jax import lax
from jax.experimental import pallas as pl
from jax.experimental.pallas import tpu as pltpu
from jax.sharding import PartitionSpec as P

MESH = pl.DeviceIdType.MESH
BF16 = jnp.bfloat16
F32 = jnp.float32
EDGE = 128
SPREAD = 256
PIECES = 4


def gelu(v):
    return 0.5 * v * (1.0 + jnp.tanh(0.7978845608028654 * (v + 0.044715 * (v * v * v))))


def remap(raw, pick):
    value = raw.astype(F32)
    found = jnp.where(pick == 1, value, 0.0)
    found = jnp.where(pick == 2, pltpu.roll(value, 1, 1), found)
    found = jnp.where(pick == 3, pltpu.roll(value, value.shape[1] - 1, 1), found)
    return found.astype(BF16)


def as_column(row):
    count = row.shape[1]
    down = lax.broadcasted_iota(jnp.int32, (count, count), 0)
    across = lax.broadcasted_iota(jnp.int32, (count, count), 1)
    return jnp.sum(jnp.where(down == across, jnp.broadcast_to(row, (count, count)), 0.0), axis=1, keepdims=True)


def kernel(
    space, chan, x_ref, top_ref, bottom_ref, w1_ref, b1_ref, w2_ref, b2_ref, hidden_ref, coarse_ref,
    padded, upper, lower, wide1, wide2, b1_all, b2_all, totals, hid, rim, even, odd, sums, result,
    x_send, x_recv, up_send, up_recv, low_send, low_recv, rim_send, rim_recv,
    own_sem, w_send, w_recv, f_send, f_recv, b_send, b_recv, h_send, h_recv, p_send, p_recv,
):
    s = lax.axis_index("space")
    j = lax.axis_index("chan")
    _, c, width = x_ref.shape
    channels = chan * c
    o = w1_ref.shape[2]
    o2 = w2_ref.shape[2]
    part = width // chan
    window = part + 2 * EDGE
    half = part // 2
    has_above = s > 0
    has_below = s < space - 1
    core = lax.rem(s, 2)
    mate = s + 1 - 2 * core

    def peer(k):
        return lax.rem(j + k, chan)

    def source(k):
        return lax.rem(j + chan - k, chan)

    def remote(src, dst, send, recv, where):
        return pltpu.make_async_remote_copy(
            src_ref=src, dst_ref=dst, send_sem=send, recv_sem=recv, device_id=where, device_id_type=MESH
        )

    barrier = pltpu.get_barrier_semaphore()
    for k in range(1, chan):
        pl.semaphore_signal(barrier, inc=1, device_id=(s, peer(k)), device_id_type=MESH)

    @pl.when(has_above)
    def _():
        pl.semaphore_signal(barrier, inc=1, device_id=(s - 1, j), device_id_type=MESH)

    @pl.when(has_below)
    def _():
        pl.semaphore_signal(barrier, inc=1, device_id=(s + 1, j), device_id_type=MESH)

    spans = ((0, EDGE), (EDGE, half), (EDGE + half, half), (EDGE + part, EDGE))

    def there(q):
        return pl.ds(spans[q][0], spans[q][1])

    def across(owner, q):
        begin = lax.rem(owner * part + width - EDGE + spans[q][0], width)
        return pl.ds(pl.multiple_of(begin, EDGE), spans[q][1])

    def x_copy(k, q):
        return remote(
            x_ref.at[:, :, across(peer(k), q)], padded.at[1:3, j, :, there(q)],
            x_send.at[k, q], x_recv.at[k, q], (s, peer(k)),
        )

    def up_copy(k, q):
        src = x_ref.at[1, :, across(j, q)] if k == 0 else padded.at[2, source(k), :, there(q)]
        return remote(src, upper.at[source(k), :, there(q)], up_send.at[k, q], up_recv.at[k, q], (s + 1, j))

    def low_copy(k, q):
        src = x_ref.at[0, :, across(j, q)] if k == 0 else padded.at[1, source(k), :, there(q)]
        return remote(src, lower.at[source(k), :, there(q)], low_send.at[k, q], low_recv.at[k, q], (s - 1, j))

    def pass_on(k, q):
        @pl.when(has_below)
        def _():
            up_copy(k, q).start()

        @pl.when(has_above)
        def _():
            low_copy(k, q).start()

    def place(which, owner, a):
        wide = (wide1, wide2)[which]
        return wide.at[:, owner, :, a * channels : (a + 1) * channels]

    def w_own(which, a):
        return pltpu.make_async_copy((w1_ref, w2_ref)[which].at[a], place(which, j, a), own_sem.at[which, a])

    def w_copy(which, a, k):
        return remote(
            (w1_ref, w2_ref)[which].at[a], place(which, j, a),
            w_send.at[which, a, k], w_recv.at[which, a, k], (s, peer(k)),
        )

    def w_pass(which, a, k):
        return remote(
            place(which, source(k), a), place(which, source(k), a),
            f_send.at[which, a, k], f_recv.at[which, a, k], (mate, j),
        )

    shares = (((0, 0), (0, 1), (1, 0)), ((0, 2), (1, 1), (1, 2)))

    def each_weight(which, mine, others):
        for side in range(2):
            @pl.when(core == side)
            def _():
                for w, a in shares[side]:
                    if w == which:
                        for k in range(1, chan):
                            mine(w, a, k)
                for w, a in shares[1 - side]:
                    if w == which:
                        for k in range(1, chan):
                            others(w, a, k)

    def nothing(w, a, k):
        pass

    def b_copy(which, k):
        ref = (b1_ref, b2_ref)[which]
        dst = (b1_all, b2_all)[which]
        return remote(ref, dst.at[j], b_send.at[which, k], b_recv.at[which, k], (s, peer(k)))

    for which in range(2):
        for a in range(3):
            w_own(which, a).start()
    pl.semaphore_wait(barrier, chan - 1 + jnp.where(has_above, 1, 0) + jnp.where(has_below, 1, 0))
    for q in range(PIECES):
        for k in range(1, chan):
            x_copy(k, q).start()
    for q in range(PIECES):
        pass_on(0, q)
    for k in range(1, chan):
        b_copy(0, k).start()
        b_copy(1, k).start()
    each_weight(0, lambda w, a, k: w_copy(w, a, k).start(), nothing)
    each_weight(1, lambda w, a, k: w_copy(w, a, k).start(), nothing)

    for q in range(PIECES):
        padded[1:3, j, :, there(q)] = x_ref[:, :, across(j, q)]
    b1_all[j] = b1_ref[...]
    b2_all[j] = b2_ref[...]

    @pl.when(s == 0)
    def _():
        upper[...] = jnp.zeros_like(upper)
        rim[...] = jnp.zeros_like(rim)

    @pl.when(s == space - 1)
    def _():
        lower[...] = jnp.zeros_like(lower)

    column = lax.rem(j * part + width - EDGE, width) + lax.broadcasted_iota(jnp.int32, (1, window), 1)
    column = jnp.where(column >= width, column - width, column)
    before = jnp.where(column == 0, width - 1, column - 1)
    after = jnp.where(column == width - 1, 0, column + 1)

    def choice(ref):
        table = jnp.concatenate([ref[:, across(j, q)] for q in range(PIECES)], axis=1)
        return jnp.where(table == column, 1, jnp.where(table == before, 2, jnp.where(table == after, 3, 0)))

    top = choice(top_ref)
    bottom = choice(bottom_ref)

    def rims(k):
        @pl.when(has_above)
        def _():
            for q in range(PIECES):
                up_copy(k, q).wait_recv()

        @pl.when(has_below)
        def _():
            for q in range(PIECES):
                low_copy(k, q).wait_recv()

        padded[0, source(k)] = remap(upper[source(k)], jnp.broadcast_to(top, (c, window)))
        padded[3, source(k)] = remap(lower[source(k)], jnp.broadcast_to(bottom, (c, window)))

    for q in range(PIECES):
        for k in range(1, chan):
            x_copy(k, q).wait_recv()
            pass_on(k, q)

    def arrived(w, a, k):
        w_copy(w, a, k).wait_recv()
        w_pass(w, a, k).start()

    each_weight(0, arrived, nothing)
    for k in range(chan):
        rims(k)
    each_weight(0, nothing, lambda w, a, k: w_pass(w, a, k).wait_recv())
    for k in range(1, chan):
        b_copy(0, k).wait_recv()
        b_copy(1, k).wait_recv()
    for a in range(3):
        w_own(0, a).wait()
    bias = jnp.concatenate([as_column(b1_all[d]) for d in range(chan)], axis=0)

    def rim_copy():
        return remote(hid.at[1], rim, rim_send, rim_recv, (s + 1, j))

    def h_copy(r, k):
        mine = pl.ds(pl.multiple_of(j * part, EDGE), part)
        return remote(
            hid.at[r, peer(k), :, EDGE : EDGE + part], hidden_ref.at[r, :, mine],
            h_send.at[r, k], h_recv.at[r, k], (s, peer(k)),
        )

    spot = lax.broadcasted_iota(jnp.int32, (SPREAD, SPREAD), 0)
    wanted = lax.broadcasted_iota(jnp.int32, (SPREAD, SPREAD), 1)
    wanted = jnp.where(wanted < SPREAD // 2, 2 * wanted, 2 * wanted - SPREAD + 1)
    picker = jnp.where(spot == wanted, 1.0, 0.0).astype(BF16)

    def split_columns(row, at):
        odd[at, :, :EDGE] = row[:, :EDGE]
        for block in range(part // SPREAD):
            first = EDGE + block * SPREAD
            both = jnp.dot(row[:, first : first + SPREAD], picker, preferred_element_type=F32).astype(BF16)
            here = block * (SPREAD // 2)
            even[at, :, here : here + SPREAD // 2] = both[:, : SPREAD // 2]
            odd[at, :, EDGE + here : EDGE + here + SPREAD // 2] = both[:, SPREAD // 2 :]

    taps = wide1[...].reshape(3 * channels, 3 * channels)
    for r in (1, 0):
        for first in range(0, window, SPREAD):
            stack = padded[r : r + 3, :, :, first : first + SPREAD].reshape(3 * channels, SPREAD)
            totals[:, first : first + SPREAD] = jnp.dot(taps, stack, preferred_element_type=F32)
        pre = (
            pltpu.roll(totals[:channels], 1, 1)
            + totals[channels : 2 * channels]
            + pltpu.roll(totals[2 * channels :], window - 1, 1)
            + bias
        )
        hid[r] = gelu(pre).astype(BF16).reshape(chan, o, window)
        if r == 1:
            @pl.when(has_below)
            def _():
                rim_copy().start()
        for k in range(1, chan):
            h_copy(r, k).start()

    own = pl.ds(pl.multiple_of(j * part, EDGE), part)
    hidden_ref[:, :, own] = hid[:, j, :, EDGE : EDGE + part]
    split_columns(hid[0].reshape(channels, window), 1)
    split_columns(hid[1].reshape(channels, window), 2)
    each_weight(1, arrived, nothing)
    each_weight(1, nothing, lambda w, a, k: w_pass(w, a, k).wait_recv())
    for a in range(3):
        w_own(1, a).wait()

    def convolved(owner, first, last):
        depth = (last - first) * channels
        lanes = slice(first * channels, last * channels)

        def product(b, data):
            return jnp.dot(wide2[b, owner, :, lanes], data, preferred_element_type=F32)

        evens = even[first:last].reshape(depth, half)
        odds = odd[first:last].reshape(depth, half + EDGE)
        shifted = pltpu.roll(product(0, odds), 1, 1)[:, EDGE:]
        return product(1, evens) + product(2, odds[:, EDGE:]) + shifted

    for k in range(chan):
        sums[k] = convolved(peer(k), 1, 3) + as_column(b2_all[peer(k)])

    @pl.when(has_above)
    def _():
        rim_copy().wait_recv()

    split_columns(remap(rim[...].reshape(channels, window), jnp.broadcast_to(top, (channels, window))), 0)

    def p_copy(k):
        mine = pl.ds(pl.multiple_of(j * half, EDGE), half)
        return remote(result.at[k], coarse_ref.at[:, mine], p_send.at[k], p_recv.at[k], (s, peer(k)))

    for k in range(1, chan):
        result[k] = gelu(sums[k] + convolved(peer(k), 0, 1)).astype(BF16)
        p_copy(k).start()
    ours = pl.ds(pl.multiple_of(j * half, EDGE), half)
    coarse_ref[:, ours] = gelu(sums[0] + convolved(j, 0, 1)).astype(BF16)

    for k in range(1, chan):
        for q in range(PIECES):
            x_copy(k, q).wait_send()
        for which in range(2):
            b_copy(which, k).wait_send()
        for r in range(2):
            h_copy(r, k).wait()
        p_copy(k).wait()

    def sent(w, a, k):
        w_copy(w, a, k).wait_send()
        w_pass(w, a, k).wait_send()

    each_weight(0, sent, nothing)
    each_weight(1, sent, nothing)

    @pl.when(has_below)
    def _():
        for k in range(chan):
            for q in range(PIECES):
                up_copy(k, q).wait_send()
        rim_copy().wait_send()

    @pl.when(has_above)
    def _():
        for k in range(chan):
            for q in range(PIECES):
                low_copy(k, q).wait_send()


def per_device(space, chan, features, top_map, bottom_map, first_weight, first_bias, second_weight, second_bias):
    _, c, rows, width = features.shape
    o, _, _, channels = first_weight.shape
    o2 = second_weight.shape[0]
    part = width // chan
    window = part + 2 * EDGE
    half = part // 2
    x = jnp.transpose(features[0], (1, 0, 2))
    w1 = jnp.transpose(first_weight, (1, 2, 0, 3))
    w2 = jnp.transpose(second_weight, (1, 2, 0, 3))
    dma = pltpu.SemaphoreType.DMA
    in_vmem = pl.BlockSpec(memory_space=pltpu.VMEM)
    anywhere = pl.BlockSpec(memory_space=pl.ANY)
    hidden, coarse = pl.pallas_call(
        functools.partial(kernel, space, chan),
        out_shape=(
            jax.ShapeDtypeStruct((rows, o, width), BF16),
            jax.ShapeDtypeStruct((o2, width // 2), BF16),
        ),
        in_specs=[in_vmem, in_vmem, in_vmem, anywhere, in_vmem, anywhere, in_vmem],
        out_specs=(in_vmem, in_vmem),
        scratch_shapes=[
            pltpu.VMEM((4, chan, c, window), BF16),
            pltpu.VMEM((chan, c, window), BF16),
            pltpu.VMEM((chan, c, window), BF16),
            pltpu.VMEM((3, chan, o, 3 * channels), BF16),
            pltpu.VMEM((3, chan, o2, 3 * channels), BF16),
            pltpu.VMEM((chan, 1, o), F32),
            pltpu.VMEM((chan, 1, o2), F32),
            pltpu.VMEM((3 * channels, window), F32),
            pltpu.VMEM((2, chan, o, window), BF16),
            pltpu.VMEM((chan, o, window), BF16),
            pltpu.VMEM((3, channels, half), BF16),
            pltpu.VMEM((3, channels, EDGE + half), BF16),
            pltpu.VMEM((chan, o2, half), F32),
            pltpu.VMEM((chan, o2, half), BF16),
            dma((chan, PIECES)),
            dma((chan, PIECES)),
            dma((chan, PIECES)),
            dma((chan, PIECES)),
            dma((chan, PIECES)),
            dma((chan, PIECES)),
            dma,
            dma,
            dma((2, 3)),
            dma((2, 3, chan)),
            dma((2, 3, chan)),
            dma((2, 3, chan)),
            dma((2, 3, chan)),
            dma((2, chan)),
            dma((2, chan)),
            dma((2, chan)),
            dma((2, chan)),
            dma((chan,)),
            dma((chan,)),
        ],
        compiler_params=pltpu.CompilerParams(
            collective_id=0, has_side_effects=True, vmem_limit_bytes=40 * 1024 * 1024
        ),
    )(x, top_map, bottom_map, w1, first_bias[None, :], w2, second_bias[None, :])
    return jnp.transpose(hidden, (1, 0, 2))[None], coarse[None, :, None, :]


def solution(mesh):
    placed = (
        P(None, "chan", "space", None),
        P("space", None),
        P("space", None),
        P("chan", None, None, None),
        P("chan"),
        P("chan", None, None, None),
        P("chan"),
    )
    return jax.shard_map(
        functools.partial(per_device, mesh.shape["space"], mesh.shape["chan"]),
        mesh=mesh,
        in_specs=placed,
        out_specs=(P(None, "chan", "space", None), P(None, "chan", "space", None)),
        check_vma=False,
    )
```

```python
import functools

import jax
import jax.numpy as jnp
from jax import lax
from jax.experimental import pallas as pl
from jax.experimental.pallas import tpu as pltpu
from jax.sharding import PartitionSpec as P

MESH = pl.DeviceIdType.MESH
BF16 = jnp.bfloat16
F32 = jnp.float32
EDGE = 128
SPREAD = 256
PIECES = 4
GROUP = 16


def gelu(v):
    return 0.5 * v * (1.0 + jnp.tanh(0.7978845608028654 * (v + 0.044715 * (v * v * v))))


def remap(raw, pick):
    value = raw.astype(F32)
    found = jnp.where(pick == 1, value, 0.0)
    found = jnp.where(pick == 2, pltpu.roll(value, 1, 1), found)
    found = jnp.where(pick == 3, pltpu.roll(value, value.shape[1] - 1, 1), found)
    return found.astype(BF16)


def remap_into(dst, src, pick):
    for g in range(0, src.shape[0], GROUP):
        rows = slice(g, g + GROUP)
        dst[rows] = remap(src[rows], jnp.broadcast_to(pick, (GROUP, pick.shape[1])))


def as_column(row):
    count = row.shape[1]
    down = lax.broadcasted_iota(jnp.int32, (count, count), 0)
    across = lax.broadcasted_iota(jnp.int32, (count, count), 1)
    return jnp.sum(jnp.where(down == across, jnp.broadcast_to(row, (count, count)), 0.0), axis=1, keepdims=True)


def kernel(
    space, chan, x_ref, top_ref, bottom_ref, w1_ref, b1_ref, w2_ref, b2_ref, hidden_ref, coarse_ref,
    padded, upper, lower, wide1, wide2, b1_all, b2_all, bias1, bias2, totals, hid, rim, fixed, even, odd,
    sums, behind, result,
    x_send, x_recv, up_send, up_recv, low_send, low_recv, rim_send, rim_recv,
    own_sem, w_send, w_recv, f_send, f_recv, b_send, b_recv, h_send, h_recv, p_send, p_recv,
):
    s = lax.axis_index("space")
    j = lax.axis_index("chan")
    _, c, width = x_ref.shape
    channels = chan * c
    o = w1_ref.shape[2]
    o2 = w2_ref.shape[2]
    part = width // chan
    window = part + 2 * EDGE
    half = part // 2
    has_above = s > 0
    has_below = s < space - 1
    core = lax.rem(s, 2)
    mate = s + 1 - 2 * core

    def peer(k):
        return lax.rem(j + k, chan)

    def source(k):
        return lax.rem(j + chan - k, chan)

    def remote(src, dst, send, recv, where):
        return pltpu.make_async_remote_copy(
            src_ref=src, dst_ref=dst, send_sem=send, recv_sem=recv, device_id=where, device_id_type=MESH
        )

    barrier = pltpu.get_barrier_semaphore()
    for k in range(1, chan):
        pl.semaphore_signal(barrier, inc=1, device_id=(s, peer(k)), device_id_type=MESH)

    @pl.when(has_above)
    def _():
        pl.semaphore_signal(barrier, inc=1, device_id=(s - 1, j), device_id_type=MESH)

    @pl.when(has_below)
    def _():
        pl.semaphore_signal(barrier, inc=1, device_id=(s + 1, j), device_id_type=MESH)

    spans = ((0, EDGE), (EDGE, half), (EDGE + half, half), (EDGE + part, EDGE))

    def there(q):
        return pl.ds(spans[q][0], spans[q][1])

    def across(owner, q):
        begin = lax.rem(owner * part + width - EDGE + spans[q][0], width)
        return pl.ds(pl.multiple_of(begin, EDGE), spans[q][1])

    def x_copy(k, q):
        return remote(
            x_ref.at[:, :, across(peer(k), q)], padded.at[1:3, j, :, there(q)],
            x_send.at[k, q], x_recv.at[k, q], (s, peer(k)),
        )

    def up_copy(k, q):
        src = x_ref.at[1, :, across(j, q)] if k == 0 else padded.at[2, source(k), :, there(q)]
        return remote(src, upper.at[source(k), :, there(q)], up_send.at[k, q], up_recv.at[k, q], (s + 1, j))

    def low_copy(k, q):
        src = x_ref.at[0, :, across(j, q)] if k == 0 else padded.at[1, source(k), :, there(q)]
        return remote(src, lower.at[source(k), :, there(q)], low_send.at[k, q], low_recv.at[k, q], (s - 1, j))

    def pass_on(k, q):
        @pl.when(has_below)
        def _():
            up_copy(k, q).start()

        @pl.when(has_above)
        def _():
            low_copy(k, q).start()

    def place(which, owner, a):
        wide = (wide1, wide2)[which]
        return wide.at[:, owner, :, a * channels : (a + 1) * channels]

    def w_own(which, a):
        return pltpu.make_async_copy((w1_ref, w2_ref)[which].at[a], place(which, j, a), own_sem.at[which, a])

    def w_copy(which, a, k):
        return remote(
            (w1_ref, w2_ref)[which].at[a], place(which, j, a),
            w_send.at[which, a, k], w_recv.at[which, a, k], (s, peer(k)),
        )

    def w_pass(which, a, k):
        return remote(
            place(which, source(k), a), place(which, source(k), a),
            f_send.at[which, a, k], f_recv.at[which, a, k], (mate, j),
        )

    shares = (((0, 0), (0, 1), (1, 0)), ((0, 2), (1, 1), (1, 2)))

    def each_weight(which, mine, others):
        for side in range(2):
            @pl.when(core == side)
            def _():
                for w, a in shares[side]:
                    if w == which:
                        for k in range(1, chan):
                            mine(w, a, k)
                for w, a in shares[1 - side]:
                    if w == which:
                        for k in range(1, chan):
                            others(w, a, k)

    def nothing(w, a, k):
        pass

    def b_copy(which, k):
        ref = (b1_ref, b2_ref)[which]
        dst = (b1_all, b2_all)[which]
        return remote(ref, dst.at[j], b_send.at[which, k], b_recv.at[which, k], (s, peer(k)))

    for which in range(2):
        for a in range(3):
            w_own(which, a).start()
    pl.semaphore_wait(barrier, chan - 1 + jnp.where(has_above, 1, 0) + jnp.where(has_below, 1, 0))
    for q in range(PIECES):
        for k in range(1, chan):
            x_copy(k, q).start()
    for q in range(PIECES):
        pass_on(0, q)
    for k in range(1, chan):
        b_copy(0, k).start()
        b_copy(1, k).start()
    each_weight(0, lambda w, a, k: w_copy(w, a, k).start(), nothing)

    for q in range(PIECES):
        padded[1:3, j, :, there(q)] = x_ref[:, :, across(j, q)]
    b1_all[j] = b1_ref[...]
    b2_all[j] = b2_ref[...]

    @pl.when(s == 0)
    def _():
        upper[...] = jnp.zeros_like(upper)
        rim[...] = jnp.zeros_like(rim)

    @pl.when(s == space - 1)
    def _():
        lower[...] = jnp.zeros_like(lower)

    column = lax.rem(j * part + width - EDGE, width) + lax.broadcasted_iota(jnp.int32, (1, window), 1)
    column = jnp.where(column >= width, column - width, column)
    before = jnp.where(column == 0, width - 1, column - 1)
    after = jnp.where(column == width - 1, 0, column + 1)

    def choice(ref):
        table = jnp.concatenate([ref[:, across(j, q)] for q in range(PIECES)], axis=1)
        return jnp.where(table == column, 1, jnp.where(table == before, 2, jnp.where(table == after, 3, 0)))

    top = choice(top_ref)
    bottom = choice(bottom_ref)

    def upper_rim(k):
        @pl.when(has_above)
        def _():
            for q in range(PIECES):
                up_copy(k, q).wait_recv()

        remap_into(padded.at[0, source(k)], upper.at[source(k)], top)

    def lower_rim(k):
        @pl.when(has_below)
        def _():
            for q in range(PIECES):
                low_copy(k, q).wait_recv()

        remap_into(padded.at[3, source(k)], lower.at[source(k)], bottom)

    lower_rim(0)
    upper_rim(0)
    for q in range(PIECES):
        for k in range(1, chan):
            x_copy(k, q).wait_recv()
            pass_on(k, q)
    each_weight(1, lambda w, a, k: w_copy(w, a, k).start(), nothing)

    def arrived(w, a, k):
        w_copy(w, a, k).wait_recv()
        w_pass(w, a, k).start()

    each_weight(0, arrived, nothing)
    each_weight(0, nothing, lambda w, a, k: w_pass(w, a, k).wait_recv())
    for a in range(3):
        w_own(0, a).wait()
    for k in range(1, chan):
        b_copy(0, k).wait_recv()
        b_copy(1, k).wait_recv()
    for d in range(chan):
        bias1[d * o : (d + 1) * o] = as_column(b1_all[d])
        bias2[d * o2 : (d + 1) * o2] = as_column(b2_all[d])

    def taps(first, last):
        return wide1[:, :, :, first * channels : last * channels].reshape(3 * channels, (last - first) * channels)

    def rows(first, last, at):
        return padded[first:last, :, :, at : at + SPREAD].reshape((last - first) * channels, SPREAD)

    for at in range(0, window, SPREAD):
        inner = rows(1, 3, at)
        for r in (1, 0):
            totals[r, :, at : at + SPREAD] = jnp.dot(taps(1 - r, 3 - r), inner, preferred_element_type=F32)

    def rim_copy():
        return remote(hid.at[1], rim, rim_send, rim_recv, (s + 1, j))

    def h_copy(r, k):
        mine = pl.ds(pl.multiple_of(j * part, EDGE), part)
        return remote(
            hid.at[r, peer(k), :, EDGE : EDGE + part], hidden_ref.at[r, :, mine],
            h_send.at[r, k], h_recv.at[r, k], (s, peer(k)),
        )

    spot = lax.broadcasted_iota(jnp.int32, (SPREAD, SPREAD), 0)
    wanted = lax.broadcasted_iota(jnp.int32, (SPREAD, SPREAD), 1)
    wanted = jnp.where(wanted < SPREAD // 2, 2 * wanted, 2 * wanted - SPREAD + 1)
    picker = jnp.where(spot == wanted, 1.0, 0.0).astype(BF16)

    def split_columns(row, at):
        odd[at, :, :EDGE] = row[:, :EDGE]
        for block in range(part // SPREAD):
            first = EDGE + block * SPREAD
            both = jnp.dot(row[:, first : first + SPREAD], picker, preferred_element_type=F32).astype(BF16)
            here = block * (SPREAD // 2)
            even[at, :, here : here + SPREAD // 2] = both[:, : SPREAD // 2]
            odd[at, :, EDGE + here : EDGE + here + SPREAD // 2] = both[:, SPREAD // 2 :]

    for r in (1, 0):
        for k in range(1, chan):
            lower_rim(k) if r == 1 else upper_rim(k)
        for at in range(0, window, SPREAD):
            outer = rows(3 * r, 3 * r + 1, at)
            totals[r, :, at : at + SPREAD] += jnp.dot(taps(2 * r, 2 * r + 1), outer, preferred_element_type=F32)
        for g in range(0, channels, GROUP):
            pre = (
                pltpu.roll(totals[r, g : g + GROUP], 1, 1)
                + totals[r, channels + g : channels + g + GROUP]
                + pltpu.roll(totals[r, 2 * channels + g : 2 * channels + g + GROUP], window - 1, 1)
                + bias1[g : g + GROUP]
            )
            hid[r, g // o, g % o : g % o + GROUP] = gelu(pre).astype(BF16)
        if r == 1:
            @pl.when(has_below)
            def _():
                rim_copy().start()
        for k in range(1, chan):
            h_copy(r, k).start()

    own = pl.ds(pl.multiple_of(j * part, EDGE), part)
    hidden_ref[:, :, own] = hid[:, j, :, EDGE : EDGE + part]
    split_columns(hid[0].reshape(channels, window), 1)
    split_columns(hid[1].reshape(channels, window), 2)
    each_weight(1, arrived, nothing)
    each_weight(1, nothing, lambda w, a, k: w_pass(w, a, k).wait_recv())
    for a in range(3):
        w_own(1, a).wait()

    def products(first, last):
        depth = (last - first) * channels
        lanes = slice(first * channels, last * channels)

        def product(b, data):
            weight = wide2[b, :, :, lanes].reshape(chan * o2, depth)
            return jnp.dot(weight, data, preferred_element_type=F32)

        odds = odd[first:last].reshape(depth, half + EDGE)
        behind[...] = product(0, odds)
        return product(1, even[first:last].reshape(depth, half)) + product(2, odds[:, EDGE:])

    def shifted(g):
        return pltpu.roll(behind[g : g + GROUP], 1, 1)[:, EDGE:]

    sums[...] = products(1, 3)
    for g in range(0, chan * o2, GROUP):
        sums[g : g + GROUP] = sums[g : g + GROUP] + shifted(g) + bias2[g : g + GROUP]

    @pl.when(has_above)
    def _():
        rim_copy().wait_recv()

    for d in range(chan):
        remap_into(fixed.at[d], rim.at[d], top)
    split_columns(fixed[...].reshape(channels, window), 0)
    sums[...] += products(0, 1)

    def p_copy(k):
        mine = pl.ds(pl.multiple_of(j * half, EDGE), half)
        return remote(result.at[peer(k)], coarse_ref.at[:, mine], p_send.at[k], p_recv.at[k], (s, peer(k)))

    for g in range(0, chan * o2, GROUP):
        result[g // o2, g % o2 : g % o2 + GROUP] = gelu(sums[g : g + GROUP] + shifted(g)).astype(BF16)
    for k in range(1, chan):
        p_copy(k).start()
    ours = pl.ds(pl.multiple_of(j * half, EDGE), half)
    coarse_ref[:, ours] = result[j]

    for k in range(1, chan):
        for q in range(PIECES):
            x_copy(k, q).wait_send()
        for which in range(2):
            b_copy(which, k).wait_send()
        for r in range(2):
            h_copy(r, k).wait()
        p_copy(k).wait()

    def sent(w, a, k):
        w_copy(w, a, k).wait_send()
        w_pass(w, a, k).wait_send()

    each_weight(0, sent, nothing)
    each_weight(1, sent, nothing)

    @pl.when(has_below)
    def _():
        for k in range(chan):
            for q in range(PIECES):
                up_copy(k, q).wait_send()
        rim_copy().wait_send()

    @pl.when(has_above)
    def _():
        for k in range(chan):
            for q in range(PIECES):
                low_copy(k, q).wait_send()


def per_device(space, chan, features, top_map, bottom_map, first_weight, first_bias, second_weight, second_bias):
    _, c, rows, width = features.shape
    o, _, _, channels = first_weight.shape
    o2 = second_weight.shape[0]
    part = width // chan
    window = part + 2 * EDGE
    half = part // 2
    x = jnp.transpose(features[0], (1, 0, 2))
    w1 = jnp.transpose(first_weight, (1, 2, 0, 3))
    w2 = jnp.transpose(second_weight, (1, 2, 0, 3))
    dma = pltpu.SemaphoreType.DMA
    in_vmem = pl.BlockSpec(memory_space=pltpu.VMEM)
    in_hbm = pl.BlockSpec(memory_space=pltpu.HBM)
    hidden, coarse = pl.pallas_call(
        functools.partial(kernel, space, chan),
        out_shape=(
            jax.ShapeDtypeStruct((rows, o, width), BF16),
            jax.ShapeDtypeStruct((o2, width // 2), BF16),
        ),
        in_specs=[in_vmem, in_vmem, in_vmem, in_hbm, in_vmem, in_hbm, in_vmem],
        out_specs=(in_vmem, in_vmem),
        scratch_shapes=[
            pltpu.VMEM((4, chan, c, window), BF16),
            pltpu.VMEM((chan, c, window), BF16),
            pltpu.VMEM((chan, c, window), BF16),
            pltpu.VMEM((3, chan, o, 3 * channels), BF16),
            pltpu.VMEM((3, chan, o2, 3 * channels), BF16),
            pltpu.VMEM((chan, 1, o), F32),
            pltpu.VMEM((chan, 1, o2), F32),
            pltpu.VMEM((channels, 1), F32),
            pltpu.VMEM((chan * o2, 1), F32),
            pltpu.VMEM((2, 3 * channels, window), F32),
            pltpu.VMEM((2, chan, o, window), BF16),
            pltpu.VMEM((chan, o, window), BF16),
            pltpu.VMEM((chan, o, window), BF16),
            pltpu.VMEM((3, channels, half), BF16),
            pltpu.VMEM((3, channels, EDGE + half), BF16),
            pltpu.VMEM((chan * o2, half), F32),
            pltpu.VMEM((chan * o2, EDGE + half), F32),
            pltpu.VMEM((chan, o2, half), BF16),
            dma((chan, PIECES)),
            dma((chan, PIECES)),
            dma((chan, PIECES)),
            dma((chan, PIECES)),
            dma((chan, PIECES)),
            dma((chan, PIECES)),
            dma,
            dma,
            dma((2, 3)),
            dma((2, 3, chan)),
            dma((2, 3, chan)),
            dma((2, 3, chan)),
            dma((2, 3, chan)),
            dma((2, chan)),
            dma((2, chan)),
            dma((2, chan)),
            dma((2, chan)),
            dma((chan,)),
            dma((chan,)),
        ],
        compiler_params=pltpu.CompilerParams(
            collective_id=0, has_side_effects=True, vmem_limit_bytes=40 * 1024 * 1024
        ),
    )(x, top_map, bottom_map, w1, first_bias[None, :], w2, second_bias[None, :])
    return jnp.transpose(hidden, (1, 0, 2))[None], coarse[None, :, None, :]


def solution(mesh):
    placed = (
        P(None, "chan", "space", None),
        P("space", None),
        P("space", None),
        P("chan", None, None, None),
        P("chan"),
        P("chan", None, None, None),
        P("chan"),
    )
    return jax.shard_map(
        functools.partial(per_device, mesh.shape["space"], mesh.shape["chan"]),
        mesh=mesh,
        in_specs=placed,
        out_specs=(P(None, "chan", "space", None), P(None, "chan", "space", None)),
        check_vma=False,
    )
```

```python
import functools

import jax
import jax.numpy as jnp
from jax import lax
from jax.experimental import pallas as pl
from jax.experimental.pallas import tpu as pltpu
from jax.sharding import PartitionSpec as P

MESH = pl.DeviceIdType.MESH
BF16 = jnp.bfloat16
F32 = jnp.float32
EDGE = 128
SPREAD = 256
PIECES = 4
GROUP = 16


def gelu(v):
    return 0.5 * v * (1.0 + jnp.tanh(0.7978845608028654 * (v + 0.044715 * (v * v * v))))


def remap(raw, pick):
    value = raw.astype(F32)
    found = jnp.where(pick == 1, value, 0.0)
    found = jnp.where(pick == 2, pltpu.roll(value, 1, 1), found)
    found = jnp.where(pick == 3, pltpu.roll(value, value.shape[1] - 1, 1), found)
    return found.astype(BF16)


def remap_into(dst, src, pick):
    for g in range(0, src.shape[0], GROUP):
        rows = slice(g, g + GROUP)
        dst[rows] = remap(src[rows], jnp.broadcast_to(pick, (GROUP, pick.shape[1])))


def as_column(row):
    count = row.shape[1]
    down = lax.broadcasted_iota(jnp.int32, (count, count), 0)
    across = lax.broadcasted_iota(jnp.int32, (count, count), 1)
    return jnp.sum(jnp.where(down == across, jnp.broadcast_to(row, (count, count)), 0.0), axis=1, keepdims=True)


def kernel(
    space, chan, x_ref, top_ref, bottom_ref, w1_ref, b1_ref, w2_ref, b2_ref, hidden_ref, coarse_ref,
    padded, upper, lower, wide1, wide2, b1_all, b2_all, bias1, bias2, totals, hid, joint, table_above, fixed, even, odd,
    sums, behind, result,
    x_send, x_recv, up_send, up_recv, low_send, low_recv, t_send, t_recv,
    own_sem, w_send, w_recv, f_send, f_recv, b_send, b_recv, h_send, h_recv, p_send, p_recv,
):
    s = lax.axis_index("space")
    j = lax.axis_index("chan")
    _, c, width = x_ref.shape
    channels = chan * c
    o = w1_ref.shape[2]
    o2 = w2_ref.shape[2]
    part = width // chan
    window = part + 2 * EDGE
    half = part // 2
    has_above = s > 0
    has_below = s < space - 1
    core = lax.rem(s, 2)
    mate = s + 1 - 2 * core

    def peer(k):
        return lax.rem(j + k, chan)

    def source(k):
        return lax.rem(j + chan - k, chan)

    def remote(src, dst, send, recv, where):
        return pltpu.make_async_remote_copy(
            src_ref=src, dst_ref=dst, send_sem=send, recv_sem=recv, device_id=where, device_id_type=MESH
        )

    barrier = pltpu.get_barrier_semaphore()
    for k in range(1, chan):
        pl.semaphore_signal(barrier, inc=1, device_id=(s, peer(k)), device_id_type=MESH)

    @pl.when(has_above)
    def _():
        pl.semaphore_signal(barrier, inc=1, device_id=(s - 1, j), device_id_type=MESH)

    @pl.when(has_below)
    def _():
        pl.semaphore_signal(barrier, inc=1, device_id=(s + 1, j), device_id_type=MESH)

    spans = ((0, EDGE), (EDGE, half), (EDGE + half, half), (EDGE + part, EDGE))

    def there(q):
        return pl.ds(spans[q][0], spans[q][1])

    def across(owner, q):
        begin = lax.rem(owner * part + width - EDGE + spans[q][0], width)
        return pl.ds(pl.multiple_of(begin, EDGE), spans[q][1])

    def x_copy(k, q):
        return remote(
            x_ref.at[:, :, across(peer(k), q)], padded.at[1:3, j, :, there(q)],
            x_send.at[k, q], x_recv.at[k, q], (s, peer(k)),
        )

    def up_copy(k, q):
        src = x_ref.at[:, :, across(j, q)] if k == 0 else padded.at[1:3, source(k), :, there(q)]
        return remote(src, upper.at[:, source(k), :, there(q)], up_send.at[k, q], up_recv.at[k, q], (s + 1, j))

    def low_copy(k, q):
        src = x_ref.at[0, :, across(j, q)] if k == 0 else padded.at[1, source(k), :, there(q)]
        return remote(src, lower.at[source(k), :, there(q)], low_send.at[k, q], low_recv.at[k, q], (s - 1, j))

    def table_copy():
        return remote(bottom_ref, table_above, t_send, t_recv, (s + 1, j))

    def pass_on(k, q):
        @pl.when(has_below)
        def _():
            up_copy(k, q).start()

        @pl.when(has_above)
        def _():
            low_copy(k, q).start()

    def place(which, owner, a):
        wide = (wide1, wide2)[which]
        return wide.at[:, owner, :, a * channels : (a + 1) * channels]

    def w_own(which, a):
        return pltpu.make_async_copy((w1_ref, w2_ref)[which].at[a], place(which, j, a), own_sem.at[which, a])

    def w_copy(which, a, k):
        return remote(
            (w1_ref, w2_ref)[which].at[a], place(which, j, a),
            w_send.at[which, a, k], w_recv.at[which, a, k], (s, peer(k)),
        )

    def w_pass(which, a, k):
        return remote(
            place(which, source(k), a), place(which, source(k), a),
            f_send.at[which, a, k], f_recv.at[which, a, k], (mate, j),
        )

    shares = (((0, 0), (0, 1), (1, 0)), ((0, 2), (1, 1), (1, 2)))

    def each_weight(which, mine, others):
        for side in range(2):
            @pl.when(core == side)
            def _():
                for w, a in shares[side]:
                    if w == which:
                        for k in range(1, chan):
                            mine(w, a, k)
                for w, a in shares[1 - side]:
                    if w == which:
                        for k in range(1, chan):
                            others(w, a, k)

    def nothing(w, a, k):
        pass

    def b_copy(which, k):
        ref = (b1_ref, b2_ref)[which]
        dst = (b1_all, b2_all)[which]
        return remote(ref, dst.at[j], b_send.at[which, k], b_recv.at[which, k], (s, peer(k)))

    for which in range(2):
        for a in range(3):
            w_own(which, a).start()
    pl.semaphore_wait(barrier, chan - 1 + jnp.where(has_above, 1, 0) + jnp.where(has_below, 1, 0))
    for q in range(PIECES):
        for k in range(1, chan):
            x_copy(k, q).start()
    for q in range(PIECES):
        pass_on(0, q)
    for k in range(1, chan):
        b_copy(0, k).start()
        b_copy(1, k).start()

    @pl.when(has_below)
    def _():
        table_copy().start()

    each_weight(0, lambda w, a, k: w_copy(w, a, k).start(), nothing)

    for q in range(PIECES):
        padded[1:3, j, :, there(q)] = x_ref[:, :, across(j, q)]
    b1_all[j] = b1_ref[...]
    b2_all[j] = b2_ref[...]

    @pl.when(s == 0)
    def _():
        upper[...] = jnp.zeros_like(upper)
        table_above[...] = jnp.zeros_like(table_above)

    @pl.when(s == space - 1)
    def _():
        lower[...] = jnp.zeros_like(lower)

    column = lax.rem(j * part + width - EDGE, width) + lax.broadcasted_iota(jnp.int32, (1, window), 1)
    column = jnp.where(column >= width, column - width, column)
    before = jnp.where(column == 0, width - 1, column - 1)
    after = jnp.where(column == width - 1, 0, column + 1)

    def choice(ref):
        table = jnp.concatenate([ref[:, across(j, q)] for q in range(PIECES)], axis=1)
        return jnp.where(table == column, 1, jnp.where(table == before, 2, jnp.where(table == after, 3, 0)))

    top = jnp.where(has_above, choice(top_ref), 0)
    bottom = choice(bottom_ref)

    def upper_rim(k):
        @pl.when(has_above)
        def _():
            for q in range(PIECES):
                up_copy(k, q).wait_recv()

        remap_into(padded.at[0, source(k)], upper.at[1, source(k)], top)

    def lower_rim(k):
        @pl.when(has_below)
        def _():
            for q in range(PIECES):
                low_copy(k, q).wait_recv()

        remap_into(padded.at[3, source(k)], lower.at[source(k)], bottom)

    lower_rim(0)
    upper_rim(0)

    @pl.when(has_above)
    def _():
        table_copy().wait_recv()

    above = choice(table_above)
    remap_into(joint.at[j], padded.at[1, j], above)
    for q in range(PIECES):
        for k in range(1, chan):
            x_copy(k, q).wait_recv()
            pass_on(k, q)
    each_weight(1, lambda w, a, k: w_copy(w, a, k).start(), nothing)

    def arrived(w, a, k):
        w_copy(w, a, k).wait_recv()
        w_pass(w, a, k).start()

    each_weight(0, arrived, nothing)
    for k in range(1, chan):
        remap_into(joint.at[source(k)], padded.at[1, source(k)], above)
    each_weight(0, nothing, lambda w, a, k: w_pass(w, a, k).wait_recv())
    for a in range(3):
        w_own(0, a).wait()
    for k in range(1, chan):
        b_copy(0, k).wait_recv()
        b_copy(1, k).wait_recv()
    for d in range(chan):
        bias1[d * o : (d + 1) * o] = as_column(b1_all[d])
        bias2[d * o2 : (d + 1) * o2] = as_column(b2_all[d])

    def taps(first, last):
        return wide1[:, :, :, first * channels : last * channels].reshape(3 * channels, (last - first) * channels)

    def rows(first, last, at):
        return padded[first:last, :, :, at : at + SPREAD].reshape((last - first) * channels, SPREAD)

    def outer(r, at):
        if r == 2:
            return upper[:, :, :, at : at + SPREAD].reshape(2 * channels, SPREAD)
        return rows(3 * r, 3 * r + 1, at)

    for at in range(0, window, SPREAD):
        inner = rows(1, 3, at)
        for r in (1, 0):
            totals[r, :, at : at + SPREAD] = jnp.dot(taps(1 - r, 3 - r), inner, preferred_element_type=F32)
        below = joint[:, :, at : at + SPREAD].reshape(channels, SPREAD)
        totals[2, :, at : at + SPREAD] = jnp.dot(taps(2, 3), below, preferred_element_type=F32)

    def h_copy(r, k):
        mine = pl.ds(pl.multiple_of(j * part, EDGE), part)
        return remote(
            hid.at[r, peer(k), :, EDGE : EDGE + part], hidden_ref.at[r, :, mine],
            h_send.at[r, k], h_recv.at[r, k], (s, peer(k)),
        )

    spot = lax.broadcasted_iota(jnp.int32, (SPREAD, SPREAD), 0)
    wanted = lax.broadcasted_iota(jnp.int32, (SPREAD, SPREAD), 1)
    wanted = jnp.where(wanted < SPREAD // 2, 2 * wanted, 2 * wanted - SPREAD + 1)
    picker = jnp.where(spot == wanted, 1.0, 0.0).astype(BF16)

    def split_columns(row, at):
        odd[at, :, :EDGE] = row[:, :EDGE]
        for block in range(part // SPREAD):
            first = EDGE + block * SPREAD
            both = jnp.dot(row[:, first : first + SPREAD], picker, preferred_element_type=F32).astype(BF16)
            here = block * (SPREAD // 2)
            even[at, :, here : here + SPREAD // 2] = both[:, : SPREAD // 2]
            odd[at, :, EDGE + here : EDGE + here + SPREAD // 2] = both[:, SPREAD // 2 :]

    for r in (1, 0, 2):
        for k in range(1, chan):
            if r == 1:
                lower_rim(k)
            if r == 0:
                upper_rim(k)
        outer_taps = (taps(0, 1), taps(2, 3), taps(0, 2))[r]
        for at in range(0, window, SPREAD):
            totals[r, :, at : at + SPREAD] += jnp.dot(outer_taps, outer(r, at), preferred_element_type=F32)
        for g in range(0, channels, GROUP):
            pre = (
                pltpu.roll(totals[r, g : g + GROUP], 1, 1)
                + totals[r, channels + g : channels + g + GROUP]
                + pltpu.roll(totals[r, 2 * channels + g : 2 * channels + g + GROUP], window - 1, 1)
                + bias1[g : g + GROUP]
            )
            row = gelu(pre).astype(BF16)
            if r == 2:
                fixed[g : g + GROUP] = remap(row, jnp.broadcast_to(top, (GROUP, window)))
            else:
                hid[r, g // o, g % o : g % o + GROUP] = row
        if r < 2:
            for k in range(1, chan):
                h_copy(r, k).start()

    own = pl.ds(pl.multiple_of(j * part, EDGE), part)
    hidden_ref[:, :, own] = hid[:, j, :, EDGE : EDGE + part]
    split_columns(hid[0].reshape(channels, window), 1)
    split_columns(hid[1].reshape(channels, window), 2)
    split_columns(fixed[...], 0)
    each_weight(1, arrived, nothing)
    each_weight(1, nothing, lambda w, a, k: w_pass(w, a, k).wait_recv())
    for a in range(3):
        w_own(1, a).wait()

    def products(first, last):
        depth = (last - first) * channels
        lanes = slice(first * channels, last * channels)

        def product(b, data):
            weight = wide2[b, :, :, lanes].reshape(chan * o2, depth)
            return jnp.dot(weight, data, preferred_element_type=F32)

        odds = odd[first:last].reshape(depth, half + EDGE)
        behind[...] = product(0, odds)
        return product(1, even[first:last].reshape(depth, half)) + product(2, odds[:, EDGE:])

    sums[...] = products(0, 3)
    piece = o2 // 2

    def p_copy(k, h):
        mine = pl.ds(pl.multiple_of(j * half, EDGE), half)
        these = slice(h * piece, (h + 1) * piece)
        return remote(
            result.at[peer(k), these], coarse_ref.at[these, mine], p_send.at[k, h], p_recv.at[k, h], (s, peer(k))
        )

    ours = pl.ds(pl.multiple_of(j * half, EDGE), half)
    for k in [*range(1, chan), 0]:
        for h in range(2):
            for g in range(h * piece, (h + 1) * piece, GROUP):
                at = pl.ds(pl.multiple_of(peer(k) * o2 + g, GROUP), GROUP)
                shifted = pltpu.roll(behind[at], 1, 1)[:, EDGE:]
                value = gelu(sums[at] + shifted + bias2[at]).astype(BF16)
                if k == 0:
                    coarse_ref[g : g + GROUP, ours] = value
                else:
                    result[peer(k), g : g + GROUP] = value
            if k > 0:
                p_copy(k, h).start()

    for k in range(1, chan):
        for q in range(PIECES):
            x_copy(k, q).wait_send()
        for which in range(2):
            b_copy(which, k).wait_send()
        for r in range(2):
            h_copy(r, k).wait()
        for h in range(2):
            p_copy(k, h).wait()

    def sent(w, a, k):
        w_copy(w, a, k).wait_send()
        w_pass(w, a, k).wait_send()

    each_weight(0, sent, nothing)
    each_weight(1, sent, nothing)

    @pl.when(has_below)
    def _():
        for k in range(chan):
            for q in range(PIECES):
                up_copy(k, q).wait_send()
        table_copy().wait_send()

    @pl.when(has_above)
    def _():
        for k in range(chan):
            for q in range(PIECES):
                low_copy(k, q).wait_send()


def per_device(space, chan, features, top_map, bottom_map, first_weight, first_bias, second_weight, second_bias):
    _, c, rows, width = features.shape
    o, _, _, channels = first_weight.shape
    o2 = second_weight.shape[0]
    part = width // chan
    window = part + 2 * EDGE
    half = part // 2
    x = jnp.transpose(features[0], (1, 0, 2))
    w1 = jnp.transpose(first_weight, (1, 2, 0, 3))
    w2 = jnp.transpose(second_weight, (1, 2, 0, 3))
    dma = pltpu.SemaphoreType.DMA
    in_vmem = pl.BlockSpec(memory_space=pltpu.VMEM)
    in_hbm = pl.BlockSpec(memory_space=pltpu.HBM)
    hidden, coarse = pl.pallas_call(
        functools.partial(kernel, space, chan),
        out_shape=(
            jax.ShapeDtypeStruct((rows, o, width), BF16),
            jax.ShapeDtypeStruct((o2, width // 2), BF16),
        ),
        in_specs=[in_vmem, in_vmem, in_vmem, in_hbm, in_vmem, in_hbm, in_vmem],
        out_specs=(in_vmem, in_vmem),
        scratch_shapes=[
            pltpu.VMEM((4, chan, c, window), BF16),
            pltpu.VMEM((2, chan, c, window), BF16),
            pltpu.VMEM((chan, c, window), BF16),
            pltpu.VMEM((3, chan, o, 3 * channels), BF16),
            pltpu.VMEM((3, chan, o2, 3 * channels), BF16),
            pltpu.VMEM((chan, 1, o), F32),
            pltpu.VMEM((chan, 1, o2), F32),
            pltpu.VMEM((channels, 1), F32),
            pltpu.VMEM((chan * o2, 1), F32),
            pltpu.VMEM((3, 3 * channels, window), F32),
            pltpu.VMEM((2, chan, o, window), BF16),
            pltpu.VMEM((chan, c, window), BF16),
            pltpu.VMEM((1, width), jnp.int32),
            pltpu.VMEM((channels, window), BF16),
            pltpu.VMEM((3, channels, half), BF16),
            pltpu.VMEM((3, channels, EDGE + half), BF16),
            pltpu.VMEM((chan * o2, half), F32),
            pltpu.VMEM((chan * o2, EDGE + half), F32),
            pltpu.VMEM((chan, o2, half), BF16),
            dma((chan, PIECES)),
            dma((chan, PIECES)),
            dma((chan, PIECES)),
            dma((chan, PIECES)),
            dma((chan, PIECES)),
            dma((chan, PIECES)),
            dma,
            dma,
            dma((2, 3)),
            dma((2, 3, chan)),
            dma((2, 3, chan)),
            dma((2, 3, chan)),
            dma((2, 3, chan)),
            dma((2, chan)),
            dma((2, chan)),
            dma((2, chan)),
            dma((2, chan)),
            dma((chan, 2)),
            dma((chan, 2)),
        ],
        compiler_params=pltpu.CompilerParams(
            collective_id=0, has_side_effects=True, vmem_limit_bytes=40 * 1024 * 1024
        ),
    )(x, top_map, bottom_map, w1, first_bias[None, :], w2, second_bias[None, :])
    return jnp.transpose(hidden, (1, 0, 2))[None], coarse[None, :, None, :]


def solution(mesh):
    placed = (
        P(None, "chan", "space", None),
        P("space", None),
        P("space", None),
        P("chan", None, None, None),
        P("chan"),
        P("chan", None, None, None),
        P("chan"),
    )
    return jax.shard_map(
        functools.partial(per_device, mesh.shape["space"], mesh.shape["chan"]),
        mesh=mesh,
        in_specs=placed,
        out_specs=(P(None, "chan", "space", None), P(None, "chan", "space", None)),
        check_vma=False,
    )
```

```python
import functools

import jax
import jax.numpy as jnp
from jax import lax
from jax.experimental import pallas as pl
from jax.experimental.pallas import tpu as pltpu
from jax.sharding import PartitionSpec as P

MESH = pl.DeviceIdType.MESH
BF16 = jnp.bfloat16
F32 = jnp.float32
EDGE = 128
SPREAD = 256
PIECES = 3
GROUP = 16


def gelu(v):
    return 0.5 * v * (1.0 + jnp.tanh(0.7978845608028654 * (v + 0.044715 * (v * v * v))))


def remap(raw, pick):
    value = raw.astype(F32)
    found = jnp.where(pick == 1, value, 0.0)
    found = jnp.where(pick == 2, pltpu.roll(value, 1, 1), found)
    found = jnp.where(pick == 3, pltpu.roll(value, value.shape[1] - 1, 1), found)
    return found.astype(BF16)


def remap_into(dst, src, pick):
    for g in range(0, src.shape[0], GROUP):
        rows = slice(g, g + GROUP)
        dst[rows] = remap(src[rows], jnp.broadcast_to(pick, (GROUP, pick.shape[1])))


def as_column(row):
    count = row.shape[1]
    down = lax.broadcasted_iota(jnp.int32, (count, count), 0)
    across = lax.broadcasted_iota(jnp.int32, (count, count), 1)
    return jnp.sum(jnp.where(down == across, jnp.broadcast_to(row, (count, count)), 0.0), axis=1, keepdims=True)


def kernel(
    space, chan, x_ref, top_ref, bottom_ref, w1_ref, b1_ref, w2_ref, b2_ref, hidden_ref, coarse_ref,
    edge, padded, upper, lower, wide1, wide2, b1_all, b2_all, bias1, bias2, totals, hid, rim, fixed, even, odd,
    sums, behind, result,
    x_send, x_recv, up_send, up_recv, low_send, low_recv, rim_send, rim_recv,
    own_sem, w_send, w_recv, f_send, f_recv, b_send, b_recv, h_send, h_recv, p_send, p_recv,
):
    s = lax.axis_index("space")
    j = lax.axis_index("chan")
    _, c, width = x_ref.shape
    channels = chan * c
    o = w1_ref.shape[2]
    o2 = w2_ref.shape[2]
    part = width // chan
    window = part + EDGE
    half = part // 2
    has_above = s > 0
    has_below = s < space - 1
    core = lax.rem(s, 2)
    mate = s + 1 - 2 * core

    def peer(k):
        return lax.rem(j + k, chan)

    def source(k):
        return lax.rem(j + chan - k, chan)

    def remote(src, dst, send, recv, where):
        return pltpu.make_async_remote_copy(
            src_ref=src, dst_ref=dst, send_sem=send, recv_sem=recv, device_id=where, device_id_type=MESH
        )

    barrier = pltpu.get_barrier_semaphore()
    for k in range(1, chan):
        pl.semaphore_signal(barrier, inc=1, device_id=(s, peer(k)), device_id_type=MESH)

    @pl.when(has_above)
    def _():
        pl.semaphore_signal(barrier, inc=1, device_id=(s - 1, j), device_id_type=MESH)

    @pl.when(has_below)
    def _():
        pl.semaphore_signal(barrier, inc=1, device_id=(s + 1, j), device_id_type=MESH)

    spans = ((0, EDGE), (EDGE, half), (EDGE + half, half))

    def there(q):
        return pl.ds(spans[q][0], spans[q][1])

    def across(owner, q):
        return pl.ds(pl.multiple_of(owner * part + (spans[q][0] - EDGE), EDGE), spans[q][1])

    def edges(owner):
        left = pl.ds(pl.multiple_of(lax.rem(owner * part + width - EDGE, width), EDGE), EDGE)
        right = pl.ds(pl.multiple_of(lax.rem(owner * part + part, width), EDGE), EDGE)
        return left, right

    def x_copy(k, q):
        src = edge.at[peer(k)] if q == 0 else x_ref.at[:, :, across(peer(k), q)]
        return remote(
            src, padded.at[1:3, j, :, there(q)], x_send.at[k, q], x_recv.at[k, q], (s, peer(k)),
        )

    def own_row(r, q):
        return edge.at[j, r] if q == 0 else x_ref.at[r, :, across(j, q)]

    def up_copy(k, q):
        src = own_row(1, q) if k == 0 else padded.at[2, source(k), :, there(q)]
        return remote(src, upper.at[source(k), :, there(q)], up_send.at[k, q], up_recv.at[k, q], (s + 1, j))

    def low_copy(k, q):
        src = own_row(0, q) if k == 0 else padded.at[1, source(k), :, there(q)]
        return remote(src, lower.at[source(k), :, there(q)], low_send.at[k, q], low_recv.at[k, q], (s - 1, j))

    def pass_on(k, q):
        @pl.when(has_below)
        def _():
            up_copy(k, q).start()

        @pl.when(has_above)
        def _():
            low_copy(k, q).start()

    def place(which, owner, a):
        wide = (wide1, wide2)[which]
        return wide.at[:, owner, :, a * channels : (a + 1) * channels]

    def w_own(which, a):
        return pltpu.make_async_copy((w1_ref, w2_ref)[which].at[a], place(which, j, a), own_sem.at[which, a])

    def w_copy(which, a, k):
        return remote(
            (w1_ref, w2_ref)[which].at[a], place(which, j, a),
            w_send.at[which, a, k], w_recv.at[which, a, k], (s, peer(k)),
        )

    def w_pass(which, a, k):
        return remote(
            place(which, source(k), a), place(which, source(k), a),
            f_send.at[which, a, k], f_recv.at[which, a, k], (mate, j),
        )

    shares = (((0, 0), (0, 1), (1, 0)), ((0, 2), (1, 1), (1, 2)))

    def each_weight(which, mine, others):
        for side in range(2):
            @pl.when(core == side)
            def _():
                for w, a in shares[side]:
                    if w == which:
                        for k in range(1, chan):
                            mine(w, a, k)
                for w, a in shares[1 - side]:
                    if w == which:
                        for k in range(1, chan):
                            others(w, a, k)

    def nothing(w, a, k):
        pass

    def b_copy(which, k):
        ref = (b1_ref, b2_ref)[which]
        dst = (b1_all, b2_all)[which]
        return remote(ref, dst.at[j], b_send.at[which, k], b_recv.at[which, k], (s, peer(k)))

    for which in range(2):
        for a in range(3):
            w_own(which, a).start()
    side = lax.broadcasted_iota(jnp.int32, (c, EDGE), 1)
    for d in range(chan):
        left, right = edges(d)
        for r in range(2):
            ahead, behind_it = x_ref[r, :, right].astype(F32), x_ref[r, :, left].astype(F32)
            edge[d, r] = jnp.where(side < EDGE // 2, ahead, behind_it).astype(BF16)
    pl.semaphore_wait(barrier, chan - 1 + jnp.where(has_above, 1, 0) + jnp.where(has_below, 1, 0))
    for q in range(PIECES):
        for k in range(1, chan):
            x_copy(k, q).start()
    for q in range(PIECES):
        pass_on(0, q)
    for k in range(1, chan):
        b_copy(0, k).start()
        b_copy(1, k).start()
    each_weight(0, lambda w, a, k: w_copy(w, a, k).start(), nothing)

    padded[1:3, j, :, there(0)] = edge[j]
    for q in range(1, PIECES):
        padded[1:3, j, :, there(q)] = x_ref[:, :, across(j, q)]
    b1_all[j] = b1_ref[...]
    b2_all[j] = b2_ref[...]

    @pl.when(s == 0)
    def _():
        upper[...] = jnp.zeros_like(upper)
        rim[...] = jnp.zeros_like(rim)

    @pl.when(s == space - 1)
    def _():
        lower[...] = jnp.zeros_like(lower)

    lane = lax.broadcasted_iota(jnp.int32, (1, window), 1)
    column = lane + jnp.where(lane < EDGE // 2, j * part + part, j * part + width - EDGE)
    column = jnp.where(column >= width, column - width, column)
    before = jnp.where(column == 0, width - 1, column - 1)
    after = jnp.where(column == width - 1, 0, column + 1)

    def choice(ref):
        left, right = edges(j)
        first = jnp.where(lane[:, :EDGE] < EDGE // 2, ref[:, right], ref[:, left])
        table = jnp.concatenate([first] + [ref[:, across(j, q)] for q in range(1, PIECES)], axis=1)
        return jnp.where(table == column, 1, jnp.where(table == before, 2, jnp.where(table == after, 3, 0)))

    top = choice(top_ref)
    bottom = choice(bottom_ref)

    def upper_rim(k):
        @pl.when(has_above)
        def _():
            for q in range(PIECES):
                up_copy(k, q).wait_recv()

        remap_into(padded.at[0, source(k)], upper.at[source(k)], top)

    def lower_rim(k):
        @pl.when(has_below)
        def _():
            for q in range(PIECES):
                low_copy(k, q).wait_recv()

        remap_into(padded.at[3, source(k)], lower.at[source(k)], bottom)

    lower_rim(0)
    upper_rim(0)
    for q in range(PIECES):
        for k in range(1, chan):
            x_copy(k, q).wait_recv()
            pass_on(k, q)
    each_weight(1, lambda w, a, k: w_copy(w, a, k).start(), nothing)

    def arrived(w, a, k):
        w_copy(w, a, k).wait_recv()
        w_pass(w, a, k).start()

    each_weight(0, arrived, nothing)
    each_weight(0, nothing, lambda w, a, k: w_pass(w, a, k).wait_recv())
    for a in range(3):
        w_own(0, a).wait()
    for k in range(1, chan):
        b_copy(0, k).wait_recv()
        b_copy(1, k).wait_recv()
    for d in range(chan):
        bias1[d * o : (d + 1) * o] = as_column(b1_all[d])
        bias2[d * o2 : (d + 1) * o2] = as_column(b2_all[d])

    def taps(first, last):
        return wide1[:, :, :, first * channels : last * channels].reshape(3 * channels, (last - first) * channels)

    def rows(first, last, here):
        return padded[first:last, :, :, here].reshape((last - first) * channels, here.stop - here.start)

    chunks = [slice(at, min(at + SPREAD, window)) for at in range(0, window, SPREAD)]
    for here in chunks:
        inner = rows(1, 3, here)
        for r in (1, 0):
            totals[r, :, here] = jnp.dot(taps(1 - r, 3 - r), inner, preferred_element_type=F32)

    def rim_copy(d):
        return remote(hid.at[1, d], rim.at[d], rim_send.at[d], rim_recv.at[d], (s + 1, j))

    def h_copy(r, k):
        mine = pl.ds(pl.multiple_of(j * part, EDGE), part)
        return remote(
            hid.at[r, peer(k), :, EDGE : EDGE + part], hidden_ref.at[r, :, mine],
            h_send.at[r, k], h_recv.at[r, k], (s, peer(k)),
        )

    spot = lax.broadcasted_iota(jnp.int32, (SPREAD, SPREAD), 0)
    wanted = lax.broadcasted_iota(jnp.int32, (SPREAD, SPREAD), 1)
    wanted = jnp.where(wanted < SPREAD // 2, 2 * wanted, 2 * wanted - SPREAD + 1)
    picker = jnp.where(spot == wanted, 1.0, 0.0).astype(BF16)

    def split_columns(row, at):
        odd[at, :, :EDGE] = row[:, :EDGE]
        for block in range(part // SPREAD):
            first = EDGE + block * SPREAD
            both = jnp.dot(row[:, first : first + SPREAD], picker, preferred_element_type=F32).astype(BF16)
            here = block * (SPREAD // 2)
            even[at, :, here : here + SPREAD // 2] = both[:, : SPREAD // 2]
            odd[at, :, EDGE + here : EDGE + here + SPREAD // 2] = both[:, SPREAD // 2 :]

    for r in (1, 0):
        for k in range(1, chan):
            lower_rim(k) if r == 1 else upper_rim(k)
        for here in chunks:
            outer = rows(3 * r, 3 * r + 1, here)
            totals[r, :, here] += jnp.dot(taps(2 * r, 2 * r + 1), outer, preferred_element_type=F32)
        for g in range(0, channels, GROUP):
            pre = (
                pltpu.roll(totals[r, g : g + GROUP], 1, 1)
                + totals[r, channels + g : channels + g + GROUP]
                + pltpu.roll(totals[r, 2 * channels + g : 2 * channels + g + GROUP], window - 1, 1)
                + bias1[g : g + GROUP]
            )
            hid[r, g // o, g % o : g % o + GROUP] = gelu(pre).astype(BF16)
            if r == 1 and (g + GROUP) % o == 0:
                @pl.when(has_below)
                def _():
                    rim_copy(g // o).start()
        for k in range(1, chan):
            h_copy(r, k).start()

    own = pl.ds(pl.multiple_of(j * part, EDGE), part)
    hidden_ref[:, :, own] = hid[:, j, :, EDGE : EDGE + part]
    split_columns(hid[0].reshape(channels, window), 1)
    split_columns(hid[1].reshape(channels, window), 2)
    each_weight(1, arrived, nothing)
    each_weight(1, nothing, lambda w, a, k: w_pass(w, a, k).wait_recv())
    for a in range(3):
        w_own(1, a).wait()

    def products(first, last):
        depth = (last - first) * channels
        lanes = slice(first * channels, last * channels)

        def product(b, data):
            weight = wide2[b, :, :, lanes].reshape(chan * o2, depth)
            return jnp.dot(weight, data, preferred_element_type=F32)

        odds = odd[first:last].reshape(depth, half + EDGE)
        behind[...] = product(0, odds)
        return product(1, even[first:last].reshape(depth, half)) + product(2, odds[:, EDGE:])

    def shifted(g):
        return pltpu.roll(behind[g : g + GROUP], 1, 1)[:, EDGE:]

    sums[...] = products(1, 3)
    for g in range(0, chan * o2, GROUP):
        sums[g : g + GROUP] = sums[g : g + GROUP] + shifted(g) + bias2[g : g + GROUP]

    for d in range(chan):
        @pl.when(has_above)
        def _():
            rim_copy(d).wait_recv()

        remap_into(fixed.at[d], rim.at[d], top)
    split_columns(fixed[...].reshape(channels, window), 0)
    sums[...] += products(0, 1)

    piece = o2 // 2

    def p_copy(k, h):
        mine = pl.ds(pl.multiple_of(j * half, EDGE), half)
        these = slice(h * piece, (h + 1) * piece)
        return remote(
            result.at[peer(k), these], coarse_ref.at[these, mine], p_send.at[k, h], p_recv.at[k, h], (s, peer(k))
        )

    ours = pl.ds(pl.multiple_of(j * half, EDGE), half)
    for k in [*range(1, chan), 0]:
        for h in range(2):
            for g in range(h * piece, (h + 1) * piece, GROUP):
                at = pl.ds(pl.multiple_of(peer(k) * o2 + g, GROUP), GROUP)
                value = gelu(sums[at] + pltpu.roll(behind[at], 1, 1)[:, EDGE:]).astype(BF16)
                if k == 0:
                    coarse_ref[g : g + GROUP, ours] = value
                else:
                    result[peer(k), g : g + GROUP] = value
            if k > 0:
                p_copy(k, h).start()

    for k in range(1, chan):
        for q in range(PIECES):
            x_copy(k, q).wait_send()
        for which in range(2):
            b_copy(which, k).wait_send()
        for r in range(2):
            h_copy(r, k).wait()
        for h in range(2):
            p_copy(k, h).wait()

    def sent(w, a, k):
        w_copy(w, a, k).wait_send()
        w_pass(w, a, k).wait_send()

    each_weight(0, sent, nothing)
    each_weight(1, sent, nothing)

    @pl.when(has_below)
    def _():
        for k in range(chan):
            for q in range(PIECES):
                up_copy(k, q).wait_send()
        for d in range(chan):
            rim_copy(d).wait_send()

    @pl.when(has_above)
    def _():
        for k in range(chan):
            for q in range(PIECES):
                low_copy(k, q).wait_send()


def per_device(space, chan, features, top_map, bottom_map, first_weight, first_bias, second_weight, second_bias):
    _, c, rows, width = features.shape
    o, _, _, channels = first_weight.shape
    o2 = second_weight.shape[0]
    part = width // chan
    window = part + EDGE
    half = part // 2
    x = jnp.transpose(features[0], (1, 0, 2))
    w1 = jnp.transpose(first_weight, (1, 2, 0, 3))
    w2 = jnp.transpose(second_weight, (1, 2, 0, 3))
    dma = pltpu.SemaphoreType.DMA
    in_vmem = pl.BlockSpec(memory_space=pltpu.VMEM)
    in_hbm = pl.BlockSpec(memory_space=pltpu.HBM)
    hidden, coarse = pl.pallas_call(
        functools.partial(kernel, space, chan),
        out_shape=(
            jax.ShapeDtypeStruct((rows, o, width), BF16),
            jax.ShapeDtypeStruct((o2, width // 2), BF16),
        ),
        in_specs=[in_vmem, in_vmem, in_vmem, in_hbm, in_vmem, in_hbm, in_vmem],
        out_specs=(in_vmem, in_vmem),
        scratch_shapes=[
            pltpu.VMEM((chan, 2, c, EDGE), BF16),
            pltpu.VMEM((4, chan, c, window), BF16),
            pltpu.VMEM((chan, c, window), BF16),
            pltpu.VMEM((chan, c, window), BF16),
            pltpu.VMEM((3, chan, o, 3 * channels), BF16),
            pltpu.VMEM((3, chan, o2, 3 * channels), BF16),
            pltpu.VMEM((chan, 1, o), F32),
            pltpu.VMEM((chan, 1, o2), F32),
            pltpu.VMEM((channels, 1), F32),
            pltpu.VMEM((chan * o2, 1), F32),
            pltpu.VMEM((2, 3 * channels, window), F32),
            pltpu.VMEM((2, chan, o, window), BF16),
            pltpu.VMEM((chan, o, window), BF16),
            pltpu.VMEM((chan, o, window), BF16),
            pltpu.VMEM((3, channels, half), BF16),
            pltpu.VMEM((3, channels, EDGE + half), BF16),
            pltpu.VMEM((chan * o2, half), F32),
            pltpu.VMEM((chan * o2, EDGE + half), F32),
            pltpu.VMEM((chan, o2, half), BF16),
            dma((chan, PIECES)),
            dma((chan, PIECES)),
            dma((chan, PIECES)),
            dma((chan, PIECES)),
            dma((chan, PIECES)),
            dma((chan, PIECES)),
            dma((chan,)),
            dma((chan,)),
            dma((2, 3)),
            dma((2, 3, chan)),
            dma((2, 3, chan)),
            dma((2, 3, chan)),
            dma((2, 3, chan)),
            dma((2, chan)),
            dma((2, chan)),
            dma((2, chan)),
            dma((2, chan)),
            dma((chan, 2)),
            dma((chan, 2)),
        ],
        compiler_params=pltpu.CompilerParams(
            collective_id=0, has_side_effects=True, vmem_limit_bytes=40 * 1024 * 1024
        ),
    )(x, top_map, bottom_map, w1, first_bias[None, :], w2, second_bias[None, :])
    return jnp.transpose(hidden, (1, 0, 2))[None], coarse[None, :, None, :]


def solution(mesh):
    placed = (
        P(None, "chan", "space", None),
        P("space", None),
        P("space", None),
        P("chan", None, None, None),
        P("chan"),
        P("chan", None, None, None),
        P("chan"),
    )
    return jax.shard_map(
        functools.partial(per_device, mesh.shape["space"], mesh.shape["chan"]),
        mesh=mesh,
        in_specs=placed,
        out_specs=(P(None, "chan", "space", None), P(None, "chan", "space", None)),
        check_vma=False,
    )
```

```python
import functools

import jax
import jax.numpy as jnp
from jax import lax
from jax.experimental import pallas as pl
from jax.experimental.pallas import tpu as pltpu
from jax.sharding import PartitionSpec as P

MESH = pl.DeviceIdType.MESH
BF16 = jnp.bfloat16
F32 = jnp.float32
EDGE = 128
SPREAD = 256
PIECES = 3
GROUP = 16
RIM = 4


def gelu(v):
    return 0.5 * v * (1.0 + jnp.tanh(0.7978845608028654 * (v + 0.044715 * (v * v * v))))


def remap(raw, pick):
    value = raw.astype(F32)
    found = jnp.where(pick == 1, value, 0.0)
    found = jnp.where(pick == 2, pltpu.roll(value, 1, 1), found)
    found = jnp.where(pick == 3, pltpu.roll(value, value.shape[1] - 1, 1), found)
    return found.astype(BF16)


def remap_into(dst, src, pick):
    for g in range(0, src.shape[0], GROUP):
        rows = slice(g, g + GROUP)
        dst[rows] = remap(src[rows], jnp.broadcast_to(pick, (GROUP, pick.shape[1])))


def as_column(row):
    count = row.shape[1]
    down = lax.broadcasted_iota(jnp.int32, (count, count), 0)
    across = lax.broadcasted_iota(jnp.int32, (count, count), 1)
    return jnp.sum(jnp.where(down == across, jnp.broadcast_to(row, (count, count)), 0.0), axis=1, keepdims=True)


def kernel(
    space, chan, x_ref, top_ref, bottom_ref, w1_ref, b1_ref, w2_ref, b2_ref, hidden_ref, coarse_ref,
    edge, padded, upper, lower, wide1, wide2, b1_all, b2_all, bias1, bias2, totals, hid, rim, fixed, even, odd,
    sums, behind, result,
    x_send, x_recv, up_send, up_recv, low_send, low_recv, rim_send, rim_recv,
    own_sem, w_send, w_recv, f_send, f_recv, b_send, b_recv, h_send, h_recv, p_send, p_recv,
):
    s = lax.axis_index("space")
    j = lax.axis_index("chan")
    _, c, width = x_ref.shape
    channels = chan * c
    o = w1_ref.shape[2]
    o2 = w2_ref.shape[2]
    part = width // chan
    window = part + EDGE
    half = part // 2
    has_above = s > 0
    has_below = s < space - 1
    core = lax.rem(s, 2)
    mate = s + 1 - 2 * core

    def peer(k):
        return lax.rem(j + k, chan)

    def source(k):
        return lax.rem(j + chan - k, chan)

    def remote(src, dst, send, recv, where):
        return pltpu.make_async_remote_copy(
            src_ref=src, dst_ref=dst, send_sem=send, recv_sem=recv, device_id=where, device_id_type=MESH
        )

    barrier = pltpu.get_barrier_semaphore()
    for k in range(1, chan):
        pl.semaphore_signal(barrier, inc=1, device_id=(s, peer(k)), device_id_type=MESH)

    @pl.when(has_above)
    def _():
        pl.semaphore_signal(barrier, inc=1, device_id=(s - 1, j), device_id_type=MESH)

    @pl.when(has_below)
    def _():
        pl.semaphore_signal(barrier, inc=1, device_id=(s + 1, j), device_id_type=MESH)

    spans = ((0, EDGE), (EDGE, half), (EDGE + half, half))

    def there(q):
        return pl.ds(spans[q][0], spans[q][1])

    def across(owner, q):
        return pl.ds(pl.multiple_of(owner * part + (spans[q][0] - EDGE), EDGE), spans[q][1])

    def edges(owner):
        left = pl.ds(pl.multiple_of(lax.rem(owner * part + width - EDGE, width), EDGE), EDGE)
        right = pl.ds(pl.multiple_of(lax.rem(owner * part + part, width), EDGE), EDGE)
        return left, right

    def x_copy(k, q):
        src = edge.at[peer(k)] if q == 0 else x_ref.at[:, :, across(peer(k), q)]
        return remote(
            src, padded.at[1:3, j, :, there(q)], x_send.at[k, q], x_recv.at[k, q], (s, peer(k)),
        )

    def own_row(r, q):
        return edge.at[j, r] if q == 0 else x_ref.at[r, :, across(j, q)]

    def up_copy(k, q):
        src = own_row(1, q) if k == 0 else padded.at[2, source(k), :, there(q)]
        return remote(src, upper.at[source(k), :, there(q)], up_send.at[k, q], up_recv.at[k, q], (s + 1, j))

    def low_copy(k, q):
        src = own_row(0, q) if k == 0 else padded.at[1, source(k), :, there(q)]
        return remote(src, lower.at[source(k), :, there(q)], low_send.at[k, q], low_recv.at[k, q], (s - 1, j))

    def pass_on(k, q):
        @pl.when(has_below)
        def _():
            up_copy(k, q).start()

        @pl.when(has_above)
        def _():
            low_copy(k, q).start()

    def place(which, owner, a):
        wide = (wide1, wide2)[which]
        return wide.at[:, owner, :, a * channels : (a + 1) * channels]

    def w_own(which, a):
        return pltpu.make_async_copy((w1_ref, w2_ref)[which].at[a], place(which, j, a), own_sem.at[which, a])

    def w_copy(which, a, k):
        return remote(
            (w1_ref, w2_ref)[which].at[a], place(which, j, a),
            w_send.at[which, a, k], w_recv.at[which, a, k], (s, peer(k)),
        )

    def w_pass(which, a, k):
        return remote(
            place(which, source(k), a), place(which, source(k), a),
            f_send.at[which, a, k], f_recv.at[which, a, k], (mate, j),
        )

    shares = (((0, 0), (0, 1), (1, 0)), ((0, 2), (1, 1), (1, 2)))

    def each_weight(which, mine, others):
        for side in range(2):
            @pl.when(core == side)
            def _():
                for w, a in shares[side]:
                    if w == which:
                        for k in range(1, chan):
                            mine(w, a, k)
                for w, a in shares[1 - side]:
                    if w == which:
                        for k in range(1, chan):
                            others(w, a, k)

    def nothing(w, a, k):
        pass

    def b_copy(which, k):
        ref = (b1_ref, b2_ref)[which]
        dst = (b1_all, b2_all)[which]
        return remote(ref, dst.at[j], b_send.at[which, k], b_recv.at[which, k], (s, peer(k)))

    for which in range(2):
        for a in range(3):
            w_own(which, a).start()
    side = lax.broadcasted_iota(jnp.int32, (c, EDGE), 1)
    for d in range(chan):
        left, right = edges(d)
        for r in range(2):
            ahead, behind_it = x_ref[r, :, right].astype(F32), x_ref[r, :, left].astype(F32)
            edge[d, r] = jnp.where(side < EDGE // 2, ahead, behind_it).astype(BF16)
    pl.semaphore_wait(barrier, chan - 1 + jnp.where(has_above, 1, 0) + jnp.where(has_below, 1, 0))
    for q in range(PIECES):
        for k in range(1, chan):
            x_copy(k, q).start()
    for q in range(PIECES):
        pass_on(0, q)
    for k in range(1, chan):
        b_copy(0, k).start()
        b_copy(1, k).start()
    each_weight(0, lambda w, a, k: w_copy(w, a, k).start(), nothing)

    padded[1:3, j, :, there(0)] = edge[j]
    for q in range(1, PIECES):
        padded[1:3, j, :, there(q)] = x_ref[:, :, across(j, q)]
    b1_all[j] = b1_ref[...]
    b2_all[j] = b2_ref[...]

    @pl.when(s == 0)
    def _():
        upper[...] = jnp.zeros_like(upper)
        rim[...] = jnp.zeros_like(rim)

    @pl.when(s == space - 1)
    def _():
        lower[...] = jnp.zeros_like(lower)

    lane = lax.broadcasted_iota(jnp.int32, (1, window), 1)
    column = lane + jnp.where(lane < EDGE // 2, j * part + part, j * part + width - EDGE)
    column = jnp.where(column >= width, column - width, column)
    before = jnp.where(column == 0, width - 1, column - 1)
    after = jnp.where(column == width - 1, 0, column + 1)

    def choice(ref):
        left, right = edges(j)
        first = jnp.where(lane[:, :EDGE] < EDGE // 2, ref[:, right], ref[:, left])
        table = jnp.concatenate([first] + [ref[:, across(j, q)] for q in range(1, PIECES)], axis=1)
        return jnp.where(table == column, 1, jnp.where(table == before, 2, jnp.where(table == after, 3, 0)))

    top = choice(top_ref)
    bottom = choice(bottom_ref)

    def upper_rim(k):
        @pl.when(has_above)
        def _():
            for q in range(PIECES):
                up_copy(k, q).wait_recv()

        remap_into(padded.at[0, source(k)], upper.at[source(k)], top)

    def lower_rim(k):
        @pl.when(has_below)
        def _():
            for q in range(PIECES):
                low_copy(k, q).wait_recv()

        remap_into(padded.at[3, source(k)], lower.at[source(k)], bottom)

    lower_rim(0)
    upper_rim(0)
    for q in range(PIECES):
        for k in range(1, chan):
            x_copy(k, q).wait_recv()
            pass_on(k, q)
    each_weight(1, lambda w, a, k: w_copy(w, a, k).start(), nothing)

    def arrived(w, a, k):
        w_copy(w, a, k).wait_recv()
        w_pass(w, a, k).start()

    each_weight(0, arrived, nothing)
    each_weight(0, nothing, lambda w, a, k: w_pass(w, a, k).wait_recv())
    for a in range(3):
        w_own(0, a).wait()
    for k in range(1, chan):
        b_copy(0, k).wait_recv()
        b_copy(1, k).wait_recv()
    for d in range(chan):
        bias1[d * o : (d + 1) * o] = as_column(b1_all[d])
        bias2[d * o2 : (d + 1) * o2] = as_column(b2_all[d])

    def taps(first, last):
        return wide1[:, :, :, first * channels : last * channels].reshape(3 * channels, (last - first) * channels)

    def rows(first, last, here):
        return padded[first:last, :, :, here].reshape((last - first) * channels, here.stop - here.start)

    chunks = [slice(at, min(at + SPREAD, window)) for at in range(0, window, SPREAD)]
    for here in chunks:
        inner = rows(1, 3, here)
        for r in (1, 0):
            totals[r, :, here] = jnp.dot(taps(1 - r, 3 - r), inner, preferred_element_type=F32)

    share = channels // RIM

    def rim_copy(d):
        these = slice(d * share, (d + 1) * share)
        return remote(hid.at[1, these], rim.at[these], rim_send.at[d], rim_recv.at[d], (s + 1, j))

    def h_copy(r, k):
        mine = pl.ds(pl.multiple_of(j * part, EDGE), part)
        return remote(
            hid.at[r, pl.ds(pl.multiple_of(peer(k) * o, GROUP), o), EDGE : EDGE + part], hidden_ref.at[r, :, mine],
            h_send.at[r, k], h_recv.at[r, k], (s, peer(k)),
        )

    spot = lax.broadcasted_iota(jnp.int32, (SPREAD, SPREAD), 0)
    wanted = lax.broadcasted_iota(jnp.int32, (SPREAD, SPREAD), 1)
    wanted = jnp.where(wanted < SPREAD // 2, 2 * wanted, 2 * wanted - SPREAD + 1)
    picker = jnp.where(spot == wanted, 1.0, 0.0).astype(BF16)

    def split_columns(row, at, begin):
        these = slice(begin, begin + row.shape[0])
        odd[at, these, :EDGE] = row[:, :EDGE]
        for block in range(part // SPREAD):
            first = EDGE + block * SPREAD
            both = jnp.dot(row[:, first : first + SPREAD], picker, preferred_element_type=F32).astype(BF16)
            here = block * (SPREAD // 2)
            even[at, these, here : here + SPREAD // 2] = both[:, : SPREAD // 2]
            odd[at, these, EDGE + here : EDGE + here + SPREAD // 2] = both[:, SPREAD // 2 :]

    for r in (1, 0):
        for k in range(1, chan):
            lower_rim(k) if r == 1 else upper_rim(k)
        for here in chunks:
            outer = rows(3 * r, 3 * r + 1, here)
            totals[r, :, here] += jnp.dot(taps(2 * r, 2 * r + 1), outer, preferred_element_type=F32)
        for g in range(0, channels, GROUP):
            pre = (
                pltpu.roll(totals[r, g : g + GROUP], 1, 1)
                + totals[r, channels + g : channels + g + GROUP]
                + pltpu.roll(totals[r, 2 * channels + g : 2 * channels + g + GROUP], window - 1, 1)
                + bias1[g : g + GROUP]
            )
            hid[r, g : g + GROUP] = gelu(pre).astype(BF16)
            if r == 1 and (g + GROUP) % share == 0:
                @pl.when(has_below)
                def _():
                    rim_copy(g // share).start()
        for k in range(1, chan):
            h_copy(r, k).start()

    own = pl.ds(pl.multiple_of(j * part, EDGE), part)
    hidden_ref[:, :, own] = hid[:, pl.ds(pl.multiple_of(j * o, GROUP), o), EDGE : EDGE + part]
    split_columns(hid[0], 1, 0)
    split_columns(hid[1], 2, 0)
    each_weight(1, arrived, nothing)
    each_weight(1, nothing, lambda w, a, k: w_pass(w, a, k).wait_recv())
    for a in range(3):
        w_own(1, a).wait()

    def products(first, last):
        depth = (last - first) * channels
        lanes = slice(first * channels, last * channels)

        def product(b, data):
            weight = wide2[b, :, :, lanes].reshape(chan * o2, depth)
            return jnp.dot(weight, data, preferred_element_type=F32)

        odds = odd[first:last].reshape(depth, half + EDGE)
        behind[...] = product(0, odds)
        return product(1, even[first:last].reshape(depth, half)) + product(2, odds[:, EDGE:])

    def shifted(g):
        return pltpu.roll(behind[g : g + GROUP], 1, 1)[:, EDGE:]

    sums[...] = products(1, 3)
    for g in range(0, chan * o2, GROUP):
        sums[g : g + GROUP] = sums[g : g + GROUP] + shifted(g) + bias2[g : g + GROUP]

    for d in range(RIM):
        @pl.when(has_above)
        def _():
            rim_copy(d).wait_recv()

        remap_into(fixed, rim.at[d * share : (d + 1) * share], top)
        split_columns(fixed[...], 0, d * share)

    piece = o2 // 2

    def p_copy(k, h):
        mine = pl.ds(pl.multiple_of(j * half, EDGE), half)
        these = slice(h * piece, (h + 1) * piece)
        return remote(
            result.at[peer(k), these], coarse_ref.at[these, mine], p_send.at[k, h], p_recv.at[k, h], (s, peer(k))
        )

    ours = pl.ds(pl.multiple_of(j * half, EDGE), half)
    for k in [*range(1, chan), 0]:
        owner = peer(k)
        block = pl.ds(pl.multiple_of(owner * o2, GROUP), o2)
        late = wide2[:, owner, :, :channels]
        behind[block] = jnp.dot(late[0], odd[0], preferred_element_type=F32)
        sums[block] += jnp.dot(late[1], even[0], preferred_element_type=F32) + jnp.dot(
            late[2], odd[0, :, EDGE:], preferred_element_type=F32
        )
        for h in range(2):
            for g in range(h * piece, (h + 1) * piece, GROUP):
                at = pl.ds(pl.multiple_of(peer(k) * o2 + g, GROUP), GROUP)
                value = gelu(sums[at] + pltpu.roll(behind[at], 1, 1)[:, EDGE:]).astype(BF16)
                if k == 0:
                    coarse_ref[g : g + GROUP, ours] = value
                else:
                    result[peer(k), g : g + GROUP] = value
            if k > 0:
                p_copy(k, h).start()

    for k in range(1, chan):
        for q in range(PIECES):
            x_copy(k, q).wait_send()
        for which in range(2):
            b_copy(which, k).wait_send()
        for r in range(2):
            h_copy(r, k).wait()
        for h in range(2):
            p_copy(k, h).wait()

    def sent(w, a, k):
        w_copy(w, a, k).wait_send()
        w_pass(w, a, k).wait_send()

    each_weight(0, sent, nothing)
    each_weight(1, sent, nothing)

    @pl.when(has_below)
    def _():
        for k in range(chan):
            for q in range(PIECES):
                up_copy(k, q).wait_send()
        for d in range(RIM):
            rim_copy(d).wait_send()

    @pl.when(has_above)
    def _():
        for k in range(chan):
            for q in range(PIECES):
                low_copy(k, q).wait_send()


def per_device(space, chan, features, top_map, bottom_map, first_weight, first_bias, second_weight, second_bias):
    _, c, rows, width = features.shape
    o, _, _, channels = first_weight.shape
    o2 = second_weight.shape[0]
    part = width // chan
    window = part + EDGE
    half = part // 2
    x = jnp.transpose(features[0], (1, 0, 2))
    w1 = jnp.transpose(first_weight, (1, 2, 0, 3))
    w2 = jnp.transpose(second_weight, (1, 2, 0, 3))
    dma = pltpu.SemaphoreType.DMA
    in_vmem = pl.BlockSpec(memory_space=pltpu.VMEM)
    in_hbm = pl.BlockSpec(memory_space=pltpu.HBM)
    hidden, coarse = pl.pallas_call(
        functools.partial(kernel, space, chan),
        out_shape=(
            jax.ShapeDtypeStruct((rows, o, width), BF16),
            jax.ShapeDtypeStruct((o2, width // 2), BF16),
        ),
        in_specs=[in_vmem, in_vmem, in_vmem, in_hbm, in_vmem, in_hbm, in_vmem],
        out_specs=(in_vmem, in_vmem),
        scratch_shapes=[
            pltpu.VMEM((chan, 2, c, EDGE), BF16),
            pltpu.VMEM((4, chan, c, window), BF16),
            pltpu.VMEM((chan, c, window), BF16),
            pltpu.VMEM((chan, c, window), BF16),
            pltpu.VMEM((3, chan, o, 3 * channels), BF16),
            pltpu.VMEM((3, chan, o2, 3 * channels), BF16),
            pltpu.VMEM((chan, 1, o), F32),
            pltpu.VMEM((chan, 1, o2), F32),
            pltpu.VMEM((channels, 1), F32),
            pltpu.VMEM((chan * o2, 1), F32),
            pltpu.VMEM((2, 3 * channels, window), F32),
            pltpu.VMEM((2, channels, window), BF16),
            pltpu.VMEM((channels, window), BF16),
            pltpu.VMEM((channels // RIM, window), BF16),
            pltpu.VMEM((3, channels, half), BF16),
            pltpu.VMEM((3, channels, EDGE + half), BF16),
            pltpu.VMEM((chan * o2, half), F32),
            pltpu.VMEM((chan * o2, EDGE + half), F32),
            pltpu.VMEM((chan, o2, half), BF16),
            dma((chan, PIECES)),
            dma((chan, PIECES)),
            dma((chan, PIECES)),
            dma((chan, PIECES)),
            dma((chan, PIECES)),
            dma((chan, PIECES)),
            dma((RIM,)),
            dma((RIM,)),
            dma((2, 3)),
            dma((2, 3, chan)),
            dma((2, 3, chan)),
            dma((2, 3, chan)),
            dma((2, 3, chan)),
            dma((2, chan)),
            dma((2, chan)),
            dma((2, chan)),
            dma((2, chan)),
            dma((chan, 2)),
            dma((chan, 2)),
        ],
        compiler_params=pltpu.CompilerParams(
            collective_id=0, has_side_effects=True, vmem_limit_bytes=40 * 1024 * 1024
        ),
    )(x, top_map, bottom_map, w1, first_bias[None, :], w2, second_bias[None, :])
    return jnp.transpose(hidden, (1, 0, 2))[None], coarse[None, :, None, :]


def solution(mesh):
    placed = (
        P(None, "chan", "space", None),
        P("space", None),
        P("space", None),
        P("chan", None, None, None),
        P("chan"),
        P("chan", None, None, None),
        P("chan"),
    )
    return jax.shard_map(
        functools.partial(per_device, mesh.shape["space"], mesh.shape["chan"]),
        mesh=mesh,
        in_specs=placed,
        out_specs=(P(None, "chan", "space", None), P(None, "chan", "space", None)),
        check_vma=False,
    )
```

```python
import functools

import jax
import jax.numpy as jnp
from jax import lax
from jax.experimental import pallas as pl
from jax.experimental.pallas import tpu as pltpu
from jax.sharding import PartitionSpec as P

MESH = pl.DeviceIdType.MESH
BF16 = jnp.bfloat16
F32 = jnp.float32
EDGE = 128
SPREAD = 256
PIECES = 3
GROUP = 16


def gelu(v):
    return 0.5 * v * (1.0 + jnp.tanh(0.7978845608028654 * (v + 0.044715 * (v * v * v))))


def remap(raw, pick):
    value = raw.astype(F32)
    found = jnp.where(pick == 1, value, 0.0)
    found = jnp.where(pick == 2, pltpu.roll(value, 1, 1), found)
    found = jnp.where(pick == 3, pltpu.roll(value, value.shape[1] - 1, 1), found)
    return found.astype(BF16)


def remap_into(dst, src, pick):
    for g in range(0, src.shape[0], GROUP):
        rows = slice(g, g + GROUP)
        dst[rows] = remap(src[rows], jnp.broadcast_to(pick, (GROUP, pick.shape[1])))


def as_column(row):
    count = row.shape[1]
    down = lax.broadcasted_iota(jnp.int32, (count, count), 0)
    across = lax.broadcasted_iota(jnp.int32, (count, count), 1)
    return jnp.sum(jnp.where(down == across, jnp.broadcast_to(row, (count, count)), 0.0), axis=1, keepdims=True)


def kernel(
    space, chan, x_ref, top_ref, bottom_ref, w1_ref, b1_ref, w2_ref, b2_ref, hidden_ref, coarse_ref,
    edge, padded, upper, lower, wide1, wide2, b1_all, b2_all, bias1, bias2, totals, hid, rim, fixed, even, odd,
    sums, behind, result,
    x_send, x_recv, up_send, up_recv, low_send, low_recv, rim_send, rim_recv,
    own_sem, w_send, w_recv, f_send, f_recv, b_send, b_recv, h_send, h_recv, p_send, p_recv,
):
    s = lax.axis_index("space")
    j = lax.axis_index("chan")
    _, c, width = x_ref.shape
    channels = chan * c
    o = w1_ref.shape[2]
    o2 = w2_ref.shape[2]
    part = width // chan
    window = part + EDGE
    half = part // 2
    has_above = s > 0
    has_below = s < space - 1
    core = lax.rem(s, 2)
    mate = s + 1 - 2 * core

    def peer(k):
        return lax.rem(j + k, chan)

    def source(k):
        return lax.rem(j + chan - k, chan)

    def remote(src, dst, send, recv, where):
        return pltpu.make_async_remote_copy(
            src_ref=src, dst_ref=dst, send_sem=send, recv_sem=recv, device_id=where, device_id_type=MESH
        )

    barrier = pltpu.get_barrier_semaphore()
    for k in range(1, chan):
        pl.semaphore_signal(barrier, inc=1, device_id=(s, peer(k)), device_id_type=MESH)

    @pl.when(has_above)
    def _():
        pl.semaphore_signal(barrier, inc=1, device_id=(s - 1, j), device_id_type=MESH)

    @pl.when(has_below)
    def _():
        pl.semaphore_signal(barrier, inc=1, device_id=(s + 1, j), device_id_type=MESH)

    spans = ((0, EDGE), (EDGE, half), (EDGE + half, half))

    def there(q):
        return pl.ds(spans[q][0], spans[q][1])

    def across(owner, q):
        return pl.ds(pl.multiple_of(owner * part + (spans[q][0] - EDGE), EDGE), spans[q][1])

    def edges(owner):
        left = pl.ds(pl.multiple_of(lax.rem(owner * part + width - EDGE, width), EDGE), EDGE)
        right = pl.ds(pl.multiple_of(lax.rem(owner * part + part, width), EDGE), EDGE)
        return left, right

    def x_copy(k, q):
        src = edge.at[peer(k)] if q == 0 else x_ref.at[:, :, across(peer(k), q)]
        return remote(
            src, padded.at[1:3, j, :, there(q)], x_send.at[k, q], x_recv.at[k, q], (s, peer(k)),
        )

    def own_row(r, q):
        return edge.at[j, r] if q == 0 else x_ref.at[r, :, across(j, q)]

    def up_copy(k, q):
        src = own_row(1, q) if k == 0 else padded.at[2, source(k), :, there(q)]
        return remote(src, upper.at[source(k), :, there(q)], up_send.at[k, q], up_recv.at[k, q], (s + 1, j))

    def low_copy(k, q):
        src = own_row(0, q) if k == 0 else padded.at[1, source(k), :, there(q)]
        return remote(src, lower.at[source(k), :, there(q)], low_send.at[k, q], low_recv.at[k, q], (s - 1, j))

    def pass_on(k, q):
        @pl.when(has_above)
        def _():
            low_copy(k, q).start()

        @pl.when(has_below)
        def _():
            up_copy(k, q).start()

    def place(which, owner, a):
        wide = (wide1, wide2)[which]
        return wide.at[:, owner, :, a * channels : (a + 1) * channels]

    def w_own(which, a):
        return pltpu.make_async_copy((w1_ref, w2_ref)[which].at[a], place(which, j, a), own_sem.at[which, a])

    def w_copy(which, a, k):
        return remote(
            (w1_ref, w2_ref)[which].at[a], place(which, j, a),
            w_send.at[which, a, k], w_recv.at[which, a, k], (s, peer(k)),
        )

    def w_pass(which, a, k):
        return remote(
            place(which, source(k), a), place(which, source(k), a),
            f_send.at[which, a, k], f_recv.at[which, a, k], (mate, j),
        )

    shares = (((0, 0), (0, 1), (1, 0)), ((0, 2), (1, 1), (1, 2)))

    def each_weight(which, mine, others):
        for side in range(2):
            @pl.when(core == side)
            def _():
                for w, a in shares[side]:
                    if w == which:
                        for k in range(1, chan):
                            mine(w, a, k)
                for w, a in shares[1 - side]:
                    if w == which:
                        for k in range(1, chan):
                            others(w, a, k)

    def nothing(w, a, k):
        pass

    def b_copy(which, k):
        ref = (b1_ref, b2_ref)[which]
        dst = (b1_all, b2_all)[which]
        return remote(ref, dst.at[j], b_send.at[which, k], b_recv.at[which, k], (s, peer(k)))

    for which in range(2):
        for a in range(3):
            w_own(which, a).start()
    side = lax.broadcasted_iota(jnp.int32, (c, EDGE), 1)
    for d in range(chan):
        left, right = edges(d)
        for r in range(2):
            ahead, behind_it = x_ref[r, :, right].astype(F32), x_ref[r, :, left].astype(F32)
            edge[d, r] = jnp.where(side < EDGE // 2, ahead, behind_it).astype(BF16)
    pl.semaphore_wait(barrier, chan - 1 + jnp.where(has_above, 1, 0) + jnp.where(has_below, 1, 0))
    for q in range(PIECES):
        if q == PIECES - 1:
            each_weight(0, lambda w, a, k: w_copy(w, a, k).start(), nothing)
        for k in range(1, chan):
            x_copy(k, q).start()
    for q in range(PIECES):
        pass_on(0, q)
    for k in range(1, chan):
        b_copy(0, k).start()
        b_copy(1, k).start()

    padded[1:3, j, :, there(0)] = edge[j]
    for q in range(1, PIECES):
        padded[1:3, j, :, there(q)] = x_ref[:, :, across(j, q)]
    b1_all[j] = b1_ref[...]
    b2_all[j] = b2_ref[...]

    @pl.when(s == 0)
    def _():
        upper[...] = jnp.zeros_like(upper)
        rim[...] = jnp.zeros_like(rim)

    @pl.when(s == space - 1)
    def _():
        lower[...] = jnp.zeros_like(lower)

    lane = lax.broadcasted_iota(jnp.int32, (1, window), 1)
    column = lane + jnp.where(lane < EDGE // 2, j * part + part, j * part + width - EDGE)
    column = jnp.where(column >= width, column - width, column)
    before = jnp.where(column == 0, width - 1, column - 1)
    after = jnp.where(column == width - 1, 0, column + 1)

    def choice(ref):
        left, right = edges(j)
        first = jnp.where(lane[:, :EDGE] < EDGE // 2, ref[:, right], ref[:, left])
        table = jnp.concatenate([first] + [ref[:, across(j, q)] for q in range(1, PIECES)], axis=1)
        return jnp.where(table == column, 1, jnp.where(table == before, 2, jnp.where(table == after, 3, 0)))

    top = choice(top_ref)
    bottom = choice(bottom_ref)

    def upper_rim(k):
        @pl.when(has_above)
        def _():
            for q in range(PIECES):
                up_copy(k, q).wait_recv()

        remap_into(padded.at[0, source(k)], upper.at[source(k)], top)

    def lower_rim(k):
        @pl.when(has_below)
        def _():
            for q in range(PIECES):
                low_copy(k, q).wait_recv()

        remap_into(padded.at[3, source(k)], lower.at[source(k)], bottom)

    lower_rim(0)
    upper_rim(0)
    def arrived(w, a, k):
        w_copy(w, a, k).wait_recv()
        w_pass(w, a, k).start()

    for q in range(PIECES):
        if q == PIECES - 1:
            each_weight(0, arrived, nothing)
        for k in range(1, chan):
            x_copy(k, q).wait_recv()
            pass_on(k, q)
    each_weight(1, lambda w, a, k: w_copy(w, a, k).start(), nothing)
    each_weight(0, nothing, lambda w, a, k: w_pass(w, a, k).wait_recv())
    for a in range(3):
        w_own(0, a).wait()
    for k in range(1, chan):
        b_copy(0, k).wait_recv()
        b_copy(1, k).wait_recv()
    for d in range(chan):
        bias1[d * o : (d + 1) * o] = as_column(b1_all[d])
        bias2[d * o2 : (d + 1) * o2] = as_column(b2_all[d])

    def taps(first, last):
        return wide1[:, :, :, first * channels : last * channels].reshape(3 * channels, (last - first) * channels)

    def rows(first, last, here):
        return padded[first:last, :, :, here].reshape((last - first) * channels, here.stop - here.start)

    chunks = [slice(at, min(at + SPREAD, window)) for at in range(0, window, SPREAD)]
    for here in chunks:
        inner = rows(1, 3, here)
        for r in (1, 0):
            totals[r, :, here] = jnp.dot(taps(1 - r, 3 - r), inner, preferred_element_type=F32)

    def rim_copy(d):
        return remote(hid.at[1, d], rim.at[d], rim_send.at[d], rim_recv.at[d], (s + 1, j))

    def h_copy(r, k):
        mine = pl.ds(pl.multiple_of(j * part, EDGE), part)
        return remote(
            hid.at[r, peer(k), :, EDGE : EDGE + part], hidden_ref.at[r, :, mine],
            h_send.at[r, k], h_recv.at[r, k], (s, peer(k)),
        )

    spot = lax.broadcasted_iota(jnp.int32, (SPREAD, SPREAD), 0)
    wanted = lax.broadcasted_iota(jnp.int32, (SPREAD, SPREAD), 1)
    wanted = jnp.where(wanted < SPREAD // 2, 2 * wanted, 2 * wanted - SPREAD + 1)
    picker = jnp.where(spot == wanted, 1.0, 0.0).astype(BF16)

    def split_columns(row, at):
        odd[at, :, :EDGE] = row[:, :EDGE]
        for block in range(part // SPREAD):
            first = EDGE + block * SPREAD
            both = jnp.dot(row[:, first : first + SPREAD], picker, preferred_element_type=F32).astype(BF16)
            here = block * (SPREAD // 2)
            even[at, :, here : here + SPREAD // 2] = both[:, : SPREAD // 2]
            odd[at, :, EDGE + here : EDGE + here + SPREAD // 2] = both[:, SPREAD // 2 :]

    for r in (1, 0):
        for k in range(1, chan):
            lower_rim(k) if r == 1 else upper_rim(k)
        for here in chunks:
            outer = rows(3 * r, 3 * r + 1, here)
            totals[r, :, here] += jnp.dot(taps(2 * r, 2 * r + 1), outer, preferred_element_type=F32)
        for g in range(0, channels, GROUP):
            pre = (
                pltpu.roll(totals[r, g : g + GROUP], 1, 1)
                + totals[r, channels + g : channels + g + GROUP]
                + pltpu.roll(totals[r, 2 * channels + g : 2 * channels + g + GROUP], window - 1, 1)
                + bias1[g : g + GROUP]
            )
            hid[r, g // o, g % o : g % o + GROUP] = gelu(pre).astype(BF16)
            if r == 1 and (g + GROUP) % o == 0:
                @pl.when(has_below)
                def _():
                    rim_copy(g // o).start()
        for k in range(1, chan):
            h_copy(r, k).start()

    own = pl.ds(pl.multiple_of(j * part, EDGE), part)
    hidden_ref[:, :, own] = hid[:, j, :, EDGE : EDGE + part]
    split_columns(hid[0].reshape(channels, window), 1)
    split_columns(hid[1].reshape(channels, window), 2)
    each_weight(1, arrived, nothing)
    each_weight(1, nothing, lambda w, a, k: w_pass(w, a, k).wait_recv())
    for a in range(3):
        w_own(1, a).wait()

    def products(first, last):
        depth = (last - first) * channels
        lanes = slice(first * channels, last * channels)

        def product(b, data):
            weight = wide2[b, :, :, lanes].reshape(chan * o2, depth)
            return jnp.dot(weight, data, preferred_element_type=F32)

        odds = odd[first:last].reshape(depth, half + EDGE)
        behind[...] = product(0, odds)
        return product(1, even[first:last].reshape(depth, half)) + product(2, odds[:, EDGE:])

    def shifted(g):
        return pltpu.roll(behind[g : g + GROUP], 1, 1)[:, EDGE:]

    sums[...] = products(1, 3)
    for g in range(0, chan * o2, GROUP):
        sums[g : g + GROUP] = sums[g : g + GROUP] + shifted(g) + bias2[g : g + GROUP]

    for d in range(chan):
        @pl.when(has_above)
        def _():
            rim_copy(d).wait_recv()

        remap_into(fixed.at[d], rim.at[d], top)
    split_columns(fixed[...].reshape(channels, window), 0)
    sums[...] += products(0, 1)

    piece = o2 // 2

    def p_copy(k, h):
        mine = pl.ds(pl.multiple_of(j * half, EDGE), half)
        these = slice(h * piece, (h + 1) * piece)
        return remote(
            result.at[peer(k), these], coarse_ref.at[these, mine], p_send.at[k, h], p_recv.at[k, h], (s, peer(k))
        )

    ours = pl.ds(pl.multiple_of(j * half, EDGE), half)
    for k in [*range(1, chan), 0]:
        for h in range(2):
            for g in range(h * piece, (h + 1) * piece, GROUP):
                at = pl.ds(pl.multiple_of(peer(k) * o2 + g, GROUP), GROUP)
                value = gelu(sums[at] + pltpu.roll(behind[at], 1, 1)[:, EDGE:]).astype(BF16)
                if k == 0:
                    coarse_ref[g : g + GROUP, ours] = value
                else:
                    result[peer(k), g : g + GROUP] = value
            if k > 0:
                p_copy(k, h).start()

    for k in range(1, chan):
        for q in range(PIECES):
            x_copy(k, q).wait_send()
        for which in range(2):
            b_copy(which, k).wait_send()
        for r in range(2):
            h_copy(r, k).wait()
        for h in range(2):
            p_copy(k, h).wait()

    def sent(w, a, k):
        w_copy(w, a, k).wait_send()
        w_pass(w, a, k).wait_send()

    each_weight(0, sent, nothing)
    each_weight(1, sent, nothing)

    @pl.when(has_below)
    def _():
        for k in range(chan):
            for q in range(PIECES):
                up_copy(k, q).wait_send()
        for d in range(chan):
            rim_copy(d).wait_send()

    @pl.when(has_above)
    def _():
        for k in range(chan):
            for q in range(PIECES):
                low_copy(k, q).wait_send()


def per_device(space, chan, features, top_map, bottom_map, first_weight, first_bias, second_weight, second_bias):
    _, c, rows, width = features.shape
    o, _, _, channels = first_weight.shape
    o2 = second_weight.shape[0]
    part = width // chan
    window = part + EDGE
    half = part // 2
    x = jnp.transpose(features[0], (1, 0, 2))
    w1 = jnp.transpose(first_weight, (1, 2, 0, 3))
    w2 = jnp.transpose(second_weight, (1, 2, 0, 3))
    dma = pltpu.SemaphoreType.DMA
    in_vmem = pl.BlockSpec(memory_space=pltpu.VMEM)
    in_hbm = pl.BlockSpec(memory_space=pltpu.HBM)
    hidden, coarse = pl.pallas_call(
        functools.partial(kernel, space, chan),
        out_shape=(
            jax.ShapeDtypeStruct((rows, o, width), BF16),
            jax.ShapeDtypeStruct((o2, width // 2), BF16),
        ),
        in_specs=[in_vmem, in_vmem, in_vmem, in_hbm, in_vmem, in_hbm, in_vmem],
        out_specs=(in_vmem, in_vmem),
        scratch_shapes=[
            pltpu.VMEM((chan, 2, c, EDGE), BF16),
            pltpu.VMEM((4, chan, c, window), BF16),
            pltpu.VMEM((chan, c, window), BF16),
            pltpu.VMEM((chan, c, window), BF16),
            pltpu.VMEM((3, chan, o, 3 * channels), BF16),
            pltpu.VMEM((3, chan, o2, 3 * channels), BF16),
            pltpu.VMEM((chan, 1, o), F32),
            pltpu.VMEM((chan, 1, o2), F32),
            pltpu.VMEM((channels, 1), F32),
            pltpu.VMEM((chan * o2, 1), F32),
            pltpu.VMEM((2, 3 * channels, window), F32),
            pltpu.VMEM((2, chan, o, window), BF16),
            pltpu.VMEM((chan, o, window), BF16),
            pltpu.VMEM((chan, o, window), BF16),
            pltpu.VMEM((3, channels, half), BF16),
            pltpu.VMEM((3, channels, EDGE + half), BF16),
            pltpu.VMEM((chan * o2, half), F32),
            pltpu.VMEM((chan * o2, EDGE + half), F32),
            pltpu.VMEM((chan, o2, half), BF16),
            dma((chan, PIECES)),
            dma((chan, PIECES)),
            dma((chan, PIECES)),
            dma((chan, PIECES)),
            dma((chan, PIECES)),
            dma((chan, PIECES)),
            dma((chan,)),
            dma((chan,)),
            dma((2, 3)),
            dma((2, 3, chan)),
            dma((2, 3, chan)),
            dma((2, 3, chan)),
            dma((2, 3, chan)),
            dma((2, chan)),
            dma((2, chan)),
            dma((2, chan)),
            dma((2, chan)),
            dma((chan, 2)),
            dma((chan, 2)),
        ],
        compiler_params=pltpu.CompilerParams(
            collective_id=0, has_side_effects=True, vmem_limit_bytes=40 * 1024 * 1024
        ),
    )(x, top_map, bottom_map, w1, first_bias[None, :], w2, second_bias[None, :])
    return jnp.transpose(hidden, (1, 0, 2))[None], coarse[None, :, None, :]


def solution(mesh):
    placed = (
        P(None, "chan", "space", None),
        P("space", None),
        P("space", None),
        P("chan", None, None, None),
        P("chan"),
        P("chan", None, None, None),
        P("chan"),
    )
    return jax.shard_map(
        functools.partial(per_device, mesh.shape["space"], mesh.shape["chan"]),
        mesh=mesh,
        in_specs=placed,
        out_specs=(P(None, "chan", "space", None), P(None, "chan", "space", None)),
        check_vma=False,
    )
```
